128 devices in a mesh: seq: 64 (over x_lo, z, y, core), hid: 2 (over x_hi).
Axes of the slice: x: 4 (x_hi: 2, x_lo: 2; x = x_hi * 2 + x_lo), y: 4, z: 4, core: 2. Of those that a mesh axis runs over, the one named last changes fastest.
Arguments:
- queries: bfloat16 [24576, 3072], P('seq', 'hid'), may hold values from -6 to 6
- keys: bfloat16 [24576, 3072], P('seq', 'hid'), may hold values from -4 to 4
- values: bfloat16 [24576, 3072], P('seq', 'hid'), may hold values from -6 to 6
- residual: bfloat16 [24576, 3072], P('seq', 'hid'), may hold values from -24 to 24
- w_in: bfloat16 [3072, 6144], P(None, 'hid'), may hold values from -0.109375 to 0.109375
- w_out: bfloat16 [6144, 3072], P('hid', 'seq'), may hold values from -0.078125 to 0.078125
- mod_scale: float32 [3072], replicated, may hold values from -0.5 to 0.5
- mod_gate: float32 [3072], replicated, may hold values from 0.5 to 1.5
- slot_tiles: int32 [64], replicated, may hold values from 0 to 63, as said below
- key_tiles: int32 [64, 27], replicated, may hold values from -1 to 63, as said below
Outputs:
- block_out: bfloat16 [24576, 3072], P('seq', 'hid')
The draws below stay inside these ranges and needn't reach their ends.
Inputs may be any that keep to these rules, and one draw needn't show every extreme that they name: slot_tiles is a permutation of the tiles of a grid of 32 x 1 x 2, tile id (t + h) * 2 + w; two tiles that differ by at most one along every grid dimension sit at most 3 slots apart. `key_tiles`: row q lists distinct tile ids, each within one step of tile q along every grid dimension, in a fixed order of the 27 offsets; column 13 is q itself; other entries are -1.
All inputs are finite; a program needn't handle non-finite values.
Results may differ from the reference program's by a relative error of at most 0.0052.
Values may be sent and summed in bfloat16 or wider, within the bound.
No kernel may reach another device: no remote copies, remote signals or barrier semaphores. Data moves between devices by JAX's collectives and lax.ppermute only.
A program may use at most 128 MiB of HBM per device.

```python
import jax
import jax.numpy as jnp
from jax import lax

D = 3072
HEADS = 24
HEAD_DIM = 128
FF = 6144
GRID_H = 1
GRID_W = 2
WINDOW = 27
TOK_DEV = 384
TILE = 384
REACH = 3
TOKENS = 24576
TILES = 64
FRAMES = 32
N_SEQ = 64


def draw_queries(key, part):
    key = jax.random.fold_in(key, 11)
    drawn = jnp.clip(jax.random.normal(key, (TOKENS, D), jnp.float32), -4.0, 4.0)
    return drawn.astype(jnp.bfloat16)


def draw_keys(key, part):
    key = jax.random.fold_in(key, 13)
    drawn = jnp.clip(jax.random.normal(key, (TOKENS, D), jnp.float32), -4.0, 4.0)
    return drawn.astype(jnp.bfloat16)


def draw_residual(key, part):
    key = jax.random.fold_in(key, 17)
    row_key = jax.random.fold_in(key, 1)
    col_key = jax.random.fold_in(key, 2)
    row_scale = jnp.exp(jax.random.uniform(row_key, (TOKENS, 1), jnp.float32, -1.2, 1.2))
    col_scale = jnp.exp(jax.random.uniform(col_key, (1, D), jnp.float32, -0.7, 0.7))
    base = jnp.clip(jax.random.normal(key, (TOKENS, D), jnp.float32), -3.0, 3.0)
    return (base * row_scale * col_scale).astype(jnp.bfloat16)


def draw_slot_tiles(key, part):
    key = jax.random.fold_in(key, 5)
    flips = jax.random.randint(key, (3,), 0, 2)
    slot_index = jnp.arange(TILES, dtype=jnp.int32)
    frame = slot_index // (GRID_H * GRID_W)
    row_pos = slot_index // GRID_W % GRID_H
    col_pos = slot_index % GRID_W
    frame = jnp.where(flips[0] == 1, FRAMES - 1 - frame, frame)
    row_pos = jnp.where(flips[1] == 1, GRID_H - 1 - row_pos, row_pos)
    col_pos = jnp.where(flips[2] == 1, GRID_W - 1 - col_pos, col_pos)
    return ((frame * GRID_H + row_pos) * GRID_W + col_pos).astype(jnp.int32)


def draw_key_tiles(key, part):
    key = jax.random.fold_in(key, 7)
    keep = jax.random.randint(key, (TILES, WINDOW), 0, 4) > 0
    tile_id = jnp.arange(TILES, dtype=jnp.int32)[:, None]
    offset = jnp.arange(WINDOW, dtype=jnp.int32)[None, :]
    frame = tile_id // (GRID_H * GRID_W) + offset // 9 - 1
    row_pos = tile_id // GRID_W % GRID_H + offset // 3 % 3 - 1
    col_pos = tile_id % GRID_W + offset % 3 - 1
    inside = (frame >= 0) & (frame < FRAMES) & (row_pos >= 0) & (row_pos < GRID_H) & (col_pos >= 0) & (col_pos < GRID_W)
    usable = inside & (keep | (offset == 13))
    return jnp.where(usable, (frame * GRID_H + row_pos) * GRID_W + col_pos, -1).astype(jnp.int32)


def block_levels(stream_key, shape, cuts, low, top_value):
    level = 1.0
    for axis_at, blocks in cuts:
        draws = jax.random.uniform(jax.random.fold_in(jax.random.fold_in(stream_key, 6), axis_at), (blocks,), jnp.float32, low / len(cuts), top_value / len(cuts))
        level = level * jnp.repeat(jnp.exp(draws), shape[axis_at] // blocks).reshape((-1,) + (1,) * (len(shape) - 1 - axis_at))
    return level


def noise(key, extent, scale, reach, shards=(), held_as=jnp.bfloat16):
    values = scale * jax.random.normal(key, extent, jnp.float32)
    if shards:
        values = values * block_levels(key, extent, shards, -0.22, 0.18)
    return jnp.clip(values, -reach, reach).astype(held_as)


def setup_inputs(seed: int = 0) -> dict:
    arg_keys = jax.random.split(jax.random.key(seed), 11)
    return {
        "queries": draw_queries(jax.random.fold_in(arg_keys[10], 71), 0),
        "keys": draw_keys(jax.random.fold_in(arg_keys[10], 71), 0),
        "values": noise(arg_keys[2], (TOKENS, D), 1.0, 6.0, ((0, 64), (1, 2))),
        "residual": draw_residual(jax.random.fold_in(arg_keys[10], 71), 0),
        "w_in": noise(arg_keys[4], (D, FF), D ** -0.5, 0.109375, ((1, 2),)),
        "w_out": noise(arg_keys[5], (FF, D), FF ** -0.5, 0.078125, ((0, 2), (1, 64))),
        "mod_scale": jnp.clip(jax.random.uniform(arg_keys[6], (D,), jnp.float32, -0.5, 0.5), -0.5, 0.5),
        "mod_gate": jnp.clip(jax.random.uniform(arg_keys[7], (D,), jnp.float32, 0.5, 1.5), 0.5, 1.5),
        "slot_tiles": draw_slot_tiles(jax.random.fold_in(arg_keys[10], 71), 0),
        "key_tiles": draw_key_tiles(jax.random.fold_in(arg_keys[10], 71), 0),
    }


def reference(queries, keys, values, residual, w_in, w_out, mod_scale, mod_gate, slot_tiles, key_tiles):
    tile_total = slot_tiles.shape[0]
    span = 2 * REACH + 1
    q_tiles = queries.reshape(tile_total, TILE, HEADS, HEAD_DIM)
    k_tiles = keys.reshape(tile_total, TILE, HEADS, HEAD_DIM)
    v_tiles = values.reshape(tile_total, TILE, HEADS, HEAD_DIM)

    def attend_tile(slot_index):
        near = slot_index - REACH + jnp.arange(span, dtype=jnp.int32)
        inside = (near >= 0) & (near < tile_total)
        near_safe = jnp.clip(near, 0, tile_total - 1).astype(jnp.int32)
        near_tiles = slot_tiles[near_safe]
        wanted = key_tiles[slot_tiles[slot_index]]
        listed = jnp.any(wanted[:, None] == near_tiles[None, :], axis=0) & inside
        k_rows = k_tiles[near_safe].reshape(span * TILE, HEADS, HEAD_DIM).astype(jnp.float32)
        v_rows = v_tiles[near_safe].reshape(span * TILE, HEADS, HEAD_DIM).astype(jnp.float32)
        row_ok = jnp.repeat(listed, TILE)
        q_rows = q_tiles[slot_index].astype(jnp.float32)
        scores = jnp.einsum('qhd,khd->hqk', q_rows, k_rows) * (1.0 / HEAD_DIM ** 0.5)
        scores = jnp.where(row_ok[None, None, :], scores, -jnp.inf)
        row_max = lax.optimization_barrier(jnp.max(scores, axis=-1, keepdims=True))
        probs = jnp.exp(scores - row_max)
        row_total = lax.optimization_barrier(jnp.sum(probs, axis=-1))
        probs_low = probs.astype(jnp.bfloat16)
        blended = jnp.einsum('hqk,khd->qhd', probs_low.astype(jnp.float32), v_rows)
        blended = blended / jnp.transpose(row_total)[:, :, None]
        return blended.reshape(TILE, D).astype(jnp.bfloat16)
    attn = lax.map(attend_tile, jnp.arange(tile_total, dtype=jnp.int32)).reshape(TOKENS, D)
    combined = (residual.astype(jnp.float32) + attn.astype(jnp.float32)).astype(jnp.bfloat16)

    def mlp_block(rows):
        wide = rows.astype(jnp.float32)
        square = lax.optimization_barrier(jnp.mean(wide * wide, axis=-1, keepdims=True))
        normed = (wide * lax.rsqrt(square + 1e-06) * (1.0 + mod_scale)).astype(jnp.bfloat16)
        inner = jnp.dot(normed, w_in, preferred_element_type=jnp.float32)
        hidden = jax.nn.gelu(inner, approximate=True).astype(jnp.bfloat16)
        return jnp.dot(hidden, w_out, preferred_element_type=jnp.float32)
    mlp = lax.map(mlp_block, combined.reshape(N_SEQ, TOK_DEV, D)).reshape(TOKENS, D)
    return (combined.astype(jnp.float32) + mod_gate * mlp).astype(jnp.bfloat16)
```

```python
import functools
import math

import jax
import jax.numpy as jnp
from jax import lax
from jax.experimental import pallas as pl
from jax.experimental.pallas import tpu as pltpu
from jax.sharding import PartitionSpec as P

HEAD_DIM = 128
TILE = 384
FEAT = 3072
HALF = 1536
UNITS = 3072
BLOCK = 384
HEAD_CHUNKS = (3, 3, 3, 3)
LOG2_SCALE = math.log2(math.e) / math.sqrt(HEAD_DIM)
AXES = ("seq", "hid")
VMEM_BYTES = 56 << 20


def place(device):
    hid = device % 2
    seq = device // 2
    return seq // 32, seq // 8 % 4, seq // 2 % 4, seq % 2, hid


def device_at(x_lo, z, y, core, hid):
    return (((x_lo * 4 + z % 4) * 4 + y % 4) * 2 + core) * 2 + hid


def moved(value, target):
    pairs = []
    for device in range(128):
        there = target(*place(device))
        if there is not None:
            pairs.append((device, there))
    return lax.ppermute(value, AXES, pairs)


def to_partner_core(x_lo, z, y, core, hid):
    return device_at(x_lo, z, y, 1 - core, hid)


def to_next_frame(x_lo, z, y, core, hid):
    chip = (x_lo * 4 + z) * 4 + y + (1 if core == 0 else -1)
    if not 0 <= chip < 32:
        return None
    return (chip * 2 + core) * 2 + hid


def along_y(x_lo, z, y, core, hid):
    return device_at(x_lo, z, y + (1 if core == 0 else -1), core, hid)


def along_z(x_lo, z, y, core, hid):
    return device_at(x_lo, z + (1 if core == 0 else -1), y, core, hid)


def along_x(x_lo, z, y, core, hid):
    return device_at(1 - x_lo, z, y, core, hid)


def to_other_hid(x_lo, z, y, core, hid):
    return device_at(x_lo, z, y, core, 1 - hid)


def attend_kernel(heads, bias_ref, q_ref, res_ref, k_ref, v_ref, other_ref, mine_ref, theirs_ref, out_ref):
    places = [(k_ref, 0, v_ref, 0), (other_ref, 0, other_ref, TILE)]
    for ref in (mine_ref, theirs_ref):
        places += [(ref, 0, ref, TILE), (ref, 2 * TILE, ref, 3 * TILE)]
    for head in range(heads):
        cols = slice(head * HEAD_DIM, (head + 1) * HEAD_DIM)
        query = q_ref[:, cols]
        scores = []
        tops = []
        for t, (key_ref, key_row, _, _) in enumerate(places):
            s = lax.dot_general(
                query,
                key_ref[key_row : key_row + TILE, cols],
                (((1,), (1,)), ((), ())),
                preferred_element_type=jnp.float32,
            )
            scores.append(s)
            tops.append(jnp.max(s, axis=-1, keepdims=True) + bias_ref[t])
        top = functools.reduce(jnp.maximum, tops) * LOG2_SCALE
        total = None
        blended = None
        for t, (_, _, val_ref, val_row) in enumerate(places):
            probs = jnp.exp2(scores[t] * LOG2_SCALE + (bias_ref[t] - top))
            row_sum = jnp.sum(probs, axis=-1, keepdims=True)
            part = jnp.dot(
                probs.astype(jnp.bfloat16),
                val_ref[val_row : val_row + TILE, cols],
                preferred_element_type=jnp.float32,
            )
            total = row_sum if total is None else total + row_sum
            blended = part if blended is None else blended + part
        attn = (blended / total).astype(jnp.bfloat16)
        out_ref[:, cols] = (
            res_ref[:, cols].astype(jnp.float32) + attn.astype(jnp.float32)
        ).astype(jnp.bfloat16)


def attend(bias, queries, residual, keys, values, other, mine, theirs, first_head, heads):
    width = heads * HEAD_DIM
    assert first_head % heads == 0
    at = first_head // heads
    tall = lambda rows: pl.BlockSpec((rows, width), lambda i: (0, 0))
    full = pl.BlockSpec((TILE, width), lambda i: (0, at))
    return pl.pallas_call(
        functools.partial(attend_kernel, heads),
        out_shape=jax.ShapeDtypeStruct((TILE, width), jnp.bfloat16),
        grid=(1,),
        in_specs=[pl.BlockSpec(memory_space=pltpu.SMEM)]
        + [full] * 4
        + [tall(2 * TILE), tall(4 * TILE), tall(4 * TILE)],
        out_specs=tall(TILE),
        compiler_params=pltpu.CompilerParams(vmem_limit_bytes=VMEM_BYTES),
        cost_estimate=pl.CostEstimate(
            flops=4 * heads * TILE * 6 * TILE * HEAD_DIM * 4,
            bytes_accessed=14 * TILE * width * 2,
            transcendentals=heads * TILE * 6 * TILE,
        ),
        name="attend",
    )(bias, queries, residual, keys, values, other, mine, theirs)


def gelu(x):
    return 0.5 * x * (1.0 + jnp.tanh(math.sqrt(2.0 / math.pi) * (x + 0.044715 * (x * x * x))))


def project_in_kernel(chunk_count, hid_ref, *refs):
    own = refs[:chunk_count]
    other = refs[chunk_count : 2 * chunk_count]
    scale_ref, w_ref, out_ref, normed_ref = refs[2 * chunk_count :]

    @pl.when(pl.program_id(0) == 0)
    def _():
        hid = hid_ref[0]
        square = None
        for ref in own + other:
            wide = ref[...].astype(jnp.float32)
            part = jnp.sum(wide * wide, axis=-1, keepdims=True)
            square = part if square is None else square + part
        factor = lax.rsqrt(square * (1.0 / FEAT) + 1e-6)
        for half, group in ((hid, own), (1 - hid, other)):
            at = 0
            for ref in group:
                width = ref.shape[1]
                cols = pl.ds(pl.multiple_of(half * HALF + at, 128), width)
                gain = 1.0 + scale_ref[:, cols]
                normed_ref[:, cols] = (ref[...].astype(jnp.float32) * factor * gain).astype(jnp.bfloat16)
                at += width

    inner = jnp.dot(normed_ref[...], w_ref[...], preferred_element_type=jnp.float32)
    out_ref[...] = gelu(inner).astype(jnp.bfloat16)


def project_in(hid, own, other, mod_scale, w_in):
    cols = 512
    whole = lambda v: pl.BlockSpec(v.shape, lambda i, h: (0, 0))
    return pl.pallas_call(
        functools.partial(project_in_kernel, len(own)),
        out_shape=jax.ShapeDtypeStruct((TILE, UNITS), jnp.bfloat16),
        grid_spec=pltpu.PrefetchScalarGridSpec(
            num_scalar_prefetch=1,
            grid=(UNITS // cols,),
            in_specs=[whole(v) for v in own + other]
            + [pl.BlockSpec((1, FEAT), lambda i, h: (0, 0)), pl.BlockSpec((FEAT, cols), lambda i, h: (0, i))],
            out_specs=pl.BlockSpec((TILE, cols), lambda i, h: (0, i)),
            scratch_shapes=[pltpu.VMEM((TILE, FEAT), jnp.bfloat16)],
        ),
        compiler_params=pltpu.CompilerParams(vmem_limit_bytes=VMEM_BYTES),
        cost_estimate=pl.CostEstimate(
            flops=2 * TILE * FEAT * UNITS, bytes_accessed=FEAT * UNITS * 2, transcendentals=TILE * UNITS
        ),
        name="project_in",
    )(hid, *own, *other, mod_scale.reshape(1, FEAT), w_in)


def project_out_kernel(flags_ref, hidden_ref, *refs):
    direct = refs[0:5]
    passed = refs[5:10]
    out_ref, w_buf, sems = refs[10:]
    from_passed = flags_ref[0]
    core = flags_ref[1]

    def copies(block, group):
        zero, mine, theirs, far_mine, far_theirs = group
        buf = w_buf.at[block]
        if block == 0:
            return [(None, [(zero, buf)])]
        if block in (1, 2):
            first, second = (mine, theirs) if block == 1 else (theirs, mine)
            return [(0, [(first, buf)]), (1, [(second, buf)])]
        low, high = buf.at[pl.ds(0, BLOCK // 2)], buf.at[pl.ds(BLOCK // 2, BLOCK // 2)]
        return [(0, [(far_mine, low), (far_theirs, high)]), (1, [(far_theirs, low), (far_mine, high)])]

    def each(block, act):
        for which, group in ((0, direct), (1, passed)):
            for needs_core, pairs in copies(block, group):
                hit = from_passed == which
                if needs_core is not None:
                    hit = hit & (core == needs_core)

                @pl.when(hit)
                def _():
                    for src, dst in pairs:
                        act(pltpu.make_async_copy(src, dst, sems.at[block]))

    for block in range(4):
        each(block, lambda c: c.start())
    for block in range(4):
        each(block, lambda c: c.wait())
        out_ref[:, block * BLOCK : (block + 1) * BLOCK] = lax.dot_general(
            hidden_ref[...], w_buf[block], (((1,), (1,)), ((), ())), preferred_element_type=jnp.float32
        ).astype(out_ref.dtype)


def project_out(flags, hidden, direct, passed, dtype):
    smem = pl.BlockSpec(memory_space=pltpu.SMEM)
    vmem = pl.BlockSpec(memory_space=pltpu.VMEM)
    hbm = pl.BlockSpec(memory_space=pl.ANY)
    return pl.pallas_call(
        project_out_kernel,
        out_shape=jax.ShapeDtypeStruct((TILE, HALF), dtype),
        in_specs=[smem, vmem] + [hbm] * 10,
        out_specs=vmem,
        scratch_shapes=[pltpu.VMEM((4, BLOCK, UNITS), jnp.bfloat16), pltpu.SemaphoreType.DMA((4,))],
        compiler_params=pltpu.CompilerParams(vmem_limit_bytes=VMEM_BYTES),
        cost_estimate=pl.CostEstimate(
            flops=2 * TILE * HALF * UNITS, bytes_accessed=HALF * UNITS * 2, transcendentals=0
        ),
        name="project_out",
    )(flags, hidden, *direct, *passed)


def spread_over_z(block, core):
    mine = moved(block, along_z)
    theirs = moved(mine, to_partner_core)
    half = BLOCK // 2
    onward = lax.dynamic_slice_in_dim(mine, core * half, half, axis=0)
    far_mine = moved(onward, along_z)
    far_theirs = moved(far_mine, to_partner_core)
    return (block, mine, theirs, far_mine, far_theirs)


def gather_w_out(w_out, x_lo, z, y, core):
    piece = w_out.T
    partner = moved(piece, to_partner_core)
    low = jnp.where(core == 0, piece, partner)
    high = jnp.where(core == 0, partner, piece)
    chip = jnp.concatenate((low, high), axis=0)
    mine = moved(chip, along_y)
    onward = lax.dynamic_slice_in_dim(mine, core * 48, 48, axis=0)
    far_mine = moved(onward, along_y)
    got = jnp.concatenate((mine, far_mine), axis=0)
    theirs = moved(got, to_partner_core)
    first = jnp.where(core == 0, got, theirs)
    second = jnp.where(core == 0, theirs, got)
    block = jnp.zeros((4, 96, UNITS), piece.dtype)
    for offset, part in (
        (0, chip),
        (1, second[:96]),
        (2, jnp.concatenate((first[96:], second[96:]), axis=0)),
        (3, first[:96]),
    ):
        block = lax.dynamic_update_slice(block, part[None], ((y + offset) % 4, 0, 0))
    block = block.reshape(BLOCK, UNITS)
    half = BLOCK // 2
    sent = lax.dynamic_slice_in_dim(block, core * half, half, axis=0)
    cross_mine = moved(sent, along_x)
    cross_theirs = moved(cross_mine, to_partner_core)
    crossed = jnp.concatenate(
        (jnp.where(core == 0, cross_mine, cross_theirs), jnp.where(core == 0, cross_theirs, cross_mine)), axis=0
    )
    return spread_over_z(block, core), spread_over_z(crossed, core)


def on_device(
    queries, keys, values, residual, w_in, w_out, mod_scale, mod_gate, slot_tiles, key_tiles
):
    seq = lax.axis_index("seq")
    hid = lax.axis_index("hid")
    core = seq % 2
    y = seq // 2 % 4
    z = seq // 8 % 4
    x_lo = seq // 32

    side = 1 - 2 * core
    slots = seq + side * jnp.array([0, 1, -2, -1, 3, 2], jnp.int32)
    inside = (slots >= 0) & (slots < slot_tiles.shape[0])
    tiles = slot_tiles[jnp.clip(slots, 0, slot_tiles.shape[0] - 1)]
    listed = jnp.any(key_tiles[slot_tiles[seq]][:, None] == tiles[None, :], axis=0)
    bias = jnp.where(listed & inside, 0.0, -jnp.inf).astype(jnp.float32)

    own = []
    first = 0
    others = []
    direct, passed = gather_w_out(w_out, x_lo, z, y, core)
    for heads in HEAD_CHUNKS:
        cols = slice(first * HEAD_DIM, (first + heads) * HEAD_DIM)
        pack = jnp.concatenate((keys[:, cols], values[:, cols]), axis=0)
        other = moved(pack, to_partner_core)
        mine = moved(jnp.concatenate((pack, other), axis=0), to_next_frame)
        theirs = moved(mine, to_partner_core)
        part = attend(bias, queries, residual, keys, values, other, mine, theirs, first, heads)
        own.append(part)
        others.append(moved(part, to_other_hid))
        first += heads

    hidden = project_in(hid.reshape(1), own, others, mod_scale, w_in)
    remote_flag = (x_lo != 1 - hid).astype(jnp.int32)
    sent = project_out(jnp.stack((remote_flag, core)), hidden, direct, passed, jnp.bfloat16)
    received = moved(sent, to_other_hid)
    kept = project_out(jnp.stack((1 - remote_flag, core)), hidden, direct, passed, jnp.float32)

    mlp = kept + received.astype(jnp.float32)
    parts = [mlp[:, i * BLOCK : (i + 1) * BLOCK] for i in (0, 2, 3, 1)]
    mlp = jnp.stack(parts, axis=0)
    mlp = jnp.concatenate((mlp, mlp), axis=0)
    mlp = lax.dynamic_slice_in_dim(mlp, (4 - z) % 4, 4, axis=0)
    mlp = jnp.transpose(mlp, (1, 0, 2)).reshape(TILE, HALF)
    gate = lax.dynamic_slice_in_dim(mod_gate, hid * HALF, HALF)
    combined = jnp.concatenate(own, axis=1)
    return (combined.astype(jnp.float32) + gate * mlp).astype(jnp.bfloat16)


def solution(mesh):
    placed = (
        P("seq", "hid"),
        P("seq", "hid"),
        P("seq", "hid"),
        P("seq", "hid"),
        P(None, "hid"),
        P("hid", "seq"),
        P(),
        P(),
        P(),
        P(),
    )
    return jax.shard_map(
        on_device, mesh=mesh, in_specs=placed, out_specs=P("seq", "hid"), check_vma=False
    )
```

```python
import functools
import math

import jax
import jax.numpy as jnp
from jax import lax
from jax.experimental import pallas as pl
from jax.experimental.pallas import tpu as pltpu
from jax.sharding import PartitionSpec as P

HEAD_DIM = 128
TILE = 384
FEAT = 3072
HALF = 1536
UNITS = 3072
PIECE = 48
BLOCK = 384
HEAD_CHUNKS = (2, 4, 4, 2)
LOG2_SCALE = math.log2(math.e) / math.sqrt(HEAD_DIM)
AXES = ("seq", "hid")
VMEM_BYTES = 56 << 20
LIGHT = pl.CostEstimate(flops=1, bytes_accessed=1, transcendentals=0)


def place(device):
    hid = device % 2
    seq = device // 2
    return seq // 32, seq // 8 % 4, seq // 2 % 4, seq % 2, hid


def device_at(x_lo, z, y, core, hid):
    return (((x_lo * 4 + z % 4) * 4 + y % 4) * 2 + core) * 2 + hid


def moved(value, target):
    pairs = []
    for device in range(128):
        there = target(*place(device))
        if there is not None:
            pairs.append((device, there))
    return lax.ppermute(value, AXES, pairs)


def after(value, *others):
    return lax.optimization_barrier((value, *others))[0]


def to_partner_core(x_lo, z, y, core, hid):
    return device_at(x_lo, z, y, 1 - core, hid)


def to_next_frame(x_lo, z, y, core, hid):
    chip = (x_lo * 4 + z) * 4 + y + (1 if core == 0 else -1)
    if not 0 <= chip < 32:
        return None
    return (chip * 2 + core) * 2 + hid


def along_y(x_lo, z, y, core, hid):
    return device_at(x_lo, z, y + (1 if core == 0 else -1), core, hid)


def along_z(x_lo, z, y, core, hid):
    return device_at(x_lo, z + (1 if core == 0 else -1), y, core, hid)


def along_x(x_lo, z, y, core, hid):
    return device_at(1 - x_lo, z, y, core, hid)


def to_other_hid(x_lo, z, y, core, hid):
    return device_at(x_lo, z, y, core, 1 - hid)


def attend_kernel(bias_ref, q_ref, res_ref, *refs):
    pairs, out_ref = refs[:3], refs[3]
    tiles = [(ref, row) for ref in pairs for row in (0, TILE)]
    for head in range(q_ref.shape[1] // HEAD_DIM):
        cols = slice(head * HEAD_DIM, (head + 1) * HEAD_DIM)
        query = q_ref[:, cols]
        scores = []
        tops = []
        for t, (ref, row) in enumerate(tiles):
            s = lax.dot_general(
                query, ref[row : row + TILE, cols], (((1,), (1,)), ((), ())), preferred_element_type=jnp.float32
            )
            scores.append(s)
            tops.append(jnp.max(s, axis=-1, keepdims=True) + bias_ref[t])
        top = functools.reduce(jnp.maximum, tops) * LOG2_SCALE
        total = None
        blended = None
        for t, (ref, row) in enumerate(tiles):
            probs = jnp.exp2(scores[t] * LOG2_SCALE + (bias_ref[t] - top))
            row_sum = jnp.sum(probs, axis=-1, keepdims=True)
            part = jnp.dot(
                probs.astype(jnp.bfloat16),
                ref[2 * TILE + row : 3 * TILE + row, cols],
                preferred_element_type=jnp.float32,
            )
            total = row_sum if total is None else total + row_sum
            blended = part if blended is None else blended + part
        attn = (blended / total).astype(jnp.bfloat16)
        out_ref[:, cols] = (res_ref[:, cols].astype(jnp.float32) + attn.astype(jnp.float32)).astype(
            jnp.bfloat16
        )


def attend(bias, queries, residual, both, mine, theirs, first, heads):
    wide = 2 * HEAD_DIM
    tall = lambda rows, at: pl.BlockSpec((rows, wide), lambda i: (0, at // 2 + i))
    return pl.pallas_call(
        attend_kernel,
        out_shape=jax.ShapeDtypeStruct((TILE, heads * HEAD_DIM), jnp.bfloat16),
        grid=(heads // 2,),
        in_specs=[pl.BlockSpec(memory_space=pltpu.SMEM)] + [tall(TILE, first)] * 2 + [tall(4 * TILE, 0)] * 3,
        out_specs=tall(TILE, 0),
        compiler_params=pltpu.CompilerParams(vmem_limit_bytes=VMEM_BYTES),
        cost_estimate=LIGHT,
        name="attend",
    )(bias, queries, residual, both, mine, theirs)


def gelu(x):
    return 0.5 * x * (1.0 + jnp.tanh(math.sqrt(2.0 / math.pi) * (x + 0.044715 * (x * x * x))))


def scaled_features(hid, groups, first, scale_ref, held_ref):
    square = None
    at = 0
    for half, group in zip((hid, 1 - hid), groups):
        feature = first
        for ref in group:
            width = ref.shape[1]
            gain = 1.0 + scale_ref[:, pl.ds(pl.multiple_of(half * HALF + feature, 128), width)]
            wide = ref[...].astype(jnp.float32)
            held_ref[:, at : at + width] = (wide * gain).astype(jnp.bfloat16)
            part = jnp.sum(wide * wide, axis=-1, keepdims=True)
            square = part if square is None else square + part
            feature += width
            at += width
    return square


def project_in_kernel(counts, blocks, first, has_earlier, is_last, hid_ref, *refs):
    own, other = refs[: counts[0]], refs[counts[0] : sum(counts)]
    scale_ref, *refs = refs[sum(counts) :]
    weights, refs = refs[: 2 * blocks], list(refs[2 * blocks :])
    acc_ref, earlier_square_ref = (refs.pop(0), refs.pop(0)) if has_earlier else (None, None)
    out_ref = refs.pop(0)
    square_ref, held_ref = refs

    @pl.when(pl.program_id(0) == 0)
    def _():
        square = scaled_features(hid_ref[0], (own, other), first, scale_ref, held_ref)
        square_ref[...] = square + earlier_square_ref[...] if has_earlier else square

    rows = weights[0].shape[0]
    inner = acc_ref[...] if has_earlier else None
    for i, w_ref in enumerate(weights):
        part = jnp.dot(held_ref[:, i * rows : (i + 1) * rows], w_ref[...], preferred_element_type=jnp.float32)
        inner = part if inner is None else inner + part
    if is_last:
        factor = lax.rsqrt(square_ref[...] * (1.0 / FEAT) + 1e-6)
        out_ref[...] = gelu(inner * factor).astype(jnp.bfloat16)
    else:
        out_ref[...] = inner


def project_in(hid, own, other, first, rows, mod_scale, w_in, earlier=None, is_last=False):
    cols = 512
    depth = sum(v.shape[1] for v in own)
    blocks = depth // rows
    assert first % rows == 0 and depth % rows == 0 and HALF % rows == 0
    whole = lambda v: pl.BlockSpec(v.shape, lambda i, h: (0, 0))
    column = pl.BlockSpec((TILE, cols), lambda i, h: (0, i))
    one = jax.ShapeDtypeStruct((TILE, 1), jnp.float32)
    scale = mod_scale.reshape(1, FEAT)

    def block(half, i):
        at = first // rows + i
        return pl.BlockSpec((rows, cols), lambda j, h: ((h[0] if half == 0 else 1 - h[0]) * (HALF // rows) + at, j))

    in_specs = [whole(v) for v in own + other] + [whole(scale)]
    in_specs += [block(half, i) for half in (0, 1) for i in range(blocks)]
    operands = [*own, *other, scale] + [w_in] * (2 * blocks)
    scratch = [pltpu.VMEM((TILE, 2 * depth), jnp.bfloat16)]
    if earlier is not None:
        in_specs += [column, whole(one)]
        operands += earlier
    if is_last:
        out_shape, out_specs = jax.ShapeDtypeStruct((TILE, UNITS), jnp.bfloat16), column
        scratch.insert(0, pltpu.VMEM((TILE, 1), jnp.float32))
    else:
        out_shape = (jax.ShapeDtypeStruct((TILE, UNITS), jnp.float32), one)
        out_specs = (column, whole(one))
    return pl.pallas_call(
        functools.partial(project_in_kernel, (len(own), len(other)), blocks, first, earlier is not None, is_last),
        out_shape=out_shape,
        grid_spec=pltpu.PrefetchScalarGridSpec(
            num_scalar_prefetch=1,
            grid=(UNITS // cols,),
            in_specs=in_specs,
            out_specs=out_specs,
            scratch_shapes=scratch,
        ),
        compiler_params=pltpu.CompilerParams(vmem_limit_bytes=VMEM_BYTES),
        cost_estimate=LIGHT,
        name="project_in",
    )(hid, *operands)


def project_out_kernel(hidden_ref, w_ref, out_ref):
    out_ref[...] = lax.dot_general(
        hidden_ref[...], w_ref[...], (((1,), (1,)), ((), ())), preferred_element_type=jnp.float32
    ).astype(out_ref.dtype)


def project_out(hidden, w_rows, dtype):
    cols = 512
    return pl.pallas_call(
        project_out_kernel,
        out_shape=jax.ShapeDtypeStruct((TILE, w_rows.shape[0]), dtype),
        grid=(w_rows.shape[0] // cols,),
        in_specs=[
            pl.BlockSpec((TILE, UNITS), lambda i: (0, 0)),
            pl.BlockSpec((cols, UNITS), lambda i: (i, 0)),
        ],
        out_specs=pl.BlockSpec((TILE, cols), lambda i: (0, i)),
        compiler_params=pltpu.CompilerParams(vmem_limit_bytes=VMEM_BYTES),
        cost_estimate=LIGHT,
        name="project_out",
    )(hidden, w_rows)


FETCHED = ((0, 0), (1, 0), (1, 1), (2, 0))
BOTH = FETCHED + tuple((-back, 1 - flip) for back, flip in FETCHED)
PIECES = tuple(
    (passed, tuple((z_back, back, flip) for back, flip in content))
    for passed, z_back, content in ((0, 0, BOTH), (0, 1, BOTH), (1, 1, BOTH), (0, 2, FETCHED), (1, 2, FETCHED))
)


def project_out_pieces_kernel(where_ref, hidden_ref, *refs):
    arrays = refs[: len(PIECES)]
    out_ref, w_buf, sems = refs[len(PIECES) :]
    z, y, core = (where_ref[i] for i in range(3))
    for ref, (passed, pieces) in zip(arrays, PIECES):
        fetcher = core + passed - 2 * core * passed
        step = 1 - 2 * fetcher
        for i, (z_back, y_back, flip) in enumerate(pieces):
            block = (z - step * z_back + 4) % 4
            y_at = (y - step * y_back + 4) % 4
            core_at = fetcher + flip - 2 * fetcher * flip
            row = pl.multiple_of(block * BLOCK + y_at * (2 * PIECE) + core_at * PIECE, 16)
            pltpu.make_async_copy(
                ref.at[pl.ds(i * PIECE, PIECE)], w_buf.at[pl.ds(row, PIECE)], sems.at[block]
            ).start()
    there = 0
    for at in range(0, HALF, 512):
        while there * BLOCK < at + 512:
            block = w_buf.at[pl.ds(there * BLOCK, BLOCK)]
            pltpu.make_async_copy(block, block, sems.at[there]).wait()
            there += 1
        out_ref[:, at : at + 512] = lax.dot_general(
            hidden_ref[...],
            w_buf[at : at + 512, :],
            (((1,), (1,)), ((), ())),
            preferred_element_type=jnp.float32,
        )


def project_out_pieces(where, hidden, arrays):
    vmem = pl.BlockSpec(memory_space=pltpu.VMEM)
    return pl.pallas_call(
        project_out_pieces_kernel,
        out_shape=jax.ShapeDtypeStruct((TILE, HALF), jnp.float32),
        in_specs=[pl.BlockSpec(memory_space=pltpu.SMEM), vmem]
        + [pl.BlockSpec(memory_space=pl.ANY)] * len(PIECES),
        out_specs=vmem,
        scratch_shapes=[pltpu.VMEM((HALF, UNITS), jnp.bfloat16), pltpu.SemaphoreType.DMA((4,))],
        compiler_params=pltpu.CompilerParams(vmem_limit_bytes=VMEM_BYTES),
        cost_estimate=LIGHT,
        name="project_out_pieces",
    )(where, hidden, *arrays)


def finish_kernel(chunk_count, *refs):
    combined = refs[:chunk_count]
    kept_ref, received_ref, gate_ref, out_ref = refs[chunk_count:]
    at = 0
    for ref in combined:
        cols = slice(at, at + ref.shape[1])
        mlp = kept_ref[:, cols] + received_ref[:, cols].astype(jnp.float32)
        out_ref[:, cols] = (ref[...].astype(jnp.float32) + gate_ref[:, cols] * mlp).astype(jnp.bfloat16)
        at = cols.stop


def finish(combined, kept, received, gate):
    vmem = pl.BlockSpec(memory_space=pltpu.VMEM)
    return pl.pallas_call(
        functools.partial(finish_kernel, len(combined)),
        out_shape=jax.ShapeDtypeStruct((TILE, HALF), jnp.bfloat16),
        in_specs=[vmem] * (len(combined) + 3),
        out_specs=vmem,
        compiler_params=pltpu.CompilerParams(vmem_limit_bytes=VMEM_BYTES),
        cost_estimate=LIGHT,
        name="finish",
    )(*combined, kept, received, gate)


def on_device(
    queries, keys, values, residual, w_in, w_out, mod_scale, mod_gate, slot_tiles, key_tiles
):
    seq = lax.axis_index("seq")
    hid = lax.axis_index("hid")
    core = seq % 2
    y = seq // 2 % 4
    z = seq // 8 % 4
    x_lo = seq // 32

    side = 1 - 2 * core
    slots = seq + side * jnp.array([0, 1, -2, -1, 3, 2], jnp.int32)
    inside = (slots >= 0) & (slots < slot_tiles.shape[0])
    tiles = slot_tiles[jnp.clip(slots, 0, slot_tiles.shape[0] - 1)]
    listed = jnp.any(key_tiles[slot_tiles[seq]][:, None] == tiles[None, :], axis=0)
    bias = jnp.where(listed & inside, 0.0, -jnp.inf).astype(jnp.float32)

    counts = HEAD_CHUNKS
    starts = [sum(counts[:i]) for i in range(len(counts))]
    cols = [slice(f * HEAD_DIM, (f + n) * HEAD_DIM) for f, n in zip(starts, counts)]
    pack = lambda c: jnp.concatenate((keys[:, c], values[:, c]), axis=0)

    swap = lambda v: moved(v, to_partner_core)
    join = lambda *v: jnp.concatenate(v, axis=0)
    hid_1 = hid.reshape(1)
    mine, own, others, theirs, both = [], [], [], [], []

    def join_frame(k, v, k_other, v_other):
        both.append(join(k, k_other, v, v_other))
        mine.append(moved(both[-1], to_next_frame))
        return both[-1]

    def attend_chunk(i, *earlier):
        part = attend(
            after(bias, *earlier), queries, residual, both[i], mine[i], theirs[i], starts[i], counts[i]
        )
        own.append(part)
        return part

    own_is_first = x_lo == 1 - hid
    same = [[32 * x + i for i in range(32)] for x in (0, 1)]
    gathered = lambda v: lax.all_gather(v, "seq", axis=0, tiled=True, axis_index_groups=same)
    piece = w_out.T
    piece_x = moved(piece, along_x)
    pack_0 = after(pack(cols[0]), piece)
    other_0 = swap(pack_0)
    pack_rest = after(pack(slice(cols[1].start, HALF)), pack_0)
    other_0 = after(other_0, pack_rest)
    done = join_frame(pack_0[:TILE], pack_0[TILE:], other_0[:TILE], other_0[TILE:])
    piece_x = after(piece_x, done)
    first = jnp.where(own_is_first, piece, piece_x)
    w_remote = gathered(first)
    pack_rest = after(pack_rest, first)
    other_rest = swap(pack_rest)

    def join_chunk(i, *earlier):
        near = slice(cols[i].start - cols[1].start, cols[i].stop - cols[1].start)
        here = after(pack_rest, *earlier)
        return join_frame(here[:TILE, near], here[TILE:, near], other_rest[:TILE, near], other_rest[TILE:, near])

    done = join_chunk(1)
    mine[0] = after(mine[0], done)
    theirs.append(swap(mine[0]))
    done = join_chunk(2, mine[0])
    done = attend_chunk(0, done)
    mine[1] = after(mine[1], done)
    theirs.append(swap(mine[1]))
    done = join_chunk(3, mine[1])
    done = attend_chunk(1, done)
    others.append(moved(jnp.concatenate(own, axis=1), to_other_hid))
    mine[2] = after(mine[2], done)
    theirs.append(swap(mine[2]))
    done = attend_chunk(2, mine[2], others[0])
    others.append(moved(done, to_other_hid))
    mine[3] = after(mine[3], done)
    theirs.append(swap(mine[3]))
    earlier = project_in(after(hid_1, mine[3]), own[:2], others[:1], 0, 768, mod_scale, w_in)
    done = attend_chunk(3, earlier[1])
    others.append(moved(done, to_other_hid))
    second = after(jnp.where(own_is_first, piece_x, piece), done, w_remote)
    w_kept = gathered(second)
    hidden = project_in(
        after(hid_1, second), own[2:], others[1:], 768, 768, mod_scale, w_in, earlier, is_last=True
    )
    sent = project_out(hidden, w_remote, jnp.bfloat16)
    received = moved(sent, to_other_hid)
    kept = project_out(after(hidden, sent), w_kept, jnp.float32)
    gate = lax.dynamic_slice_in_dim(mod_gate, hid * HALF, HALF).reshape(1, HALF)
    return finish(own, kept, received, gate)


def solution(mesh):
    placed = (
        P("seq", "hid"),
        P("seq", "hid"),
        P("seq", "hid"),
        P("seq", "hid"),
        P(None, "hid"),
        P("hid", "seq"),
        P(),
        P(),
        P(),
        P(),
    )
    return jax.shard_map(
        on_device, mesh=mesh, in_specs=placed, out_specs=P("seq", "hid"), check_vma=False
    )
```

```python
import functools
import math

import jax
import jax.numpy as jnp
from jax import lax
from jax.experimental import pallas as pl
from jax.experimental.pallas import tpu as pltpu
from jax.sharding import PartitionSpec as P

HEAD_DIM = 128
TILE = 384
FEAT = 3072
HALF = 1536
UNITS = 3072
PIECE = 48
BLOCK = 384
QUARTER = 768
FRAME_CHUNKS = (4, 8)
LOG2_SCALE = math.log2(math.e) / math.sqrt(HEAD_DIM)
AXES = ("seq", "hid")
VMEM_BYTES = 56 << 20
LIGHT = pl.CostEstimate(flops=1, bytes_accessed=1, transcendentals=0)


def place(device):
    hid = device % 2
    seq = device // 2
    return seq // 32, seq // 8 % 4, seq // 2 % 4, seq % 2, hid


def device_at(x_lo, z, y, core, hid):
    return (((x_lo * 4 + z % 4) * 4 + y % 4) * 2 + core) * 2 + hid


def moved(value, target):
    pairs = []
    for device in range(128):
        there = target(*place(device))
        if there is not None:
            pairs.append((device, there))
    return lax.ppermute(value, AXES, pairs)


def after(value, *others):
    return lax.optimization_barrier((value, *others))[0]


def to_partner_core(x_lo, z, y, core, hid):
    return device_at(x_lo, z, y, 1 - core, hid)


def to_next_frame(x_lo, z, y, core, hid):
    chip = (x_lo * 4 + z) * 4 + y + (1 if core == 0 else -1)
    if not 0 <= chip < 32:
        return None
    return (chip * 2 + core) * 2 + hid


def along_y(x_lo, z, y, core, hid):
    return device_at(x_lo, z, y + (1 if core == 0 else -1), core, hid)


def along_z(x_lo, z, y, core, hid):
    return device_at(x_lo, z + (1 if core == 0 else -1), y, core, hid)


def along_x(x_lo, z, y, core, hid):
    return device_at(1 - x_lo, z, y, core, hid)


def to_other_hid(x_lo, z, y, core, hid):
    return device_at(x_lo, z, y, core, 1 - hid)


def to_other_hid_crossed(x_lo, z, y, core, hid):
    return device_at(x_lo, z, y, 1 - core, 1 - hid)


def attend_kernel(bias_ref, q_ref, res_ref, *refs):
    pairs, out_ref = refs[:3], refs[3]
    tiles = [(ref, row) for ref in pairs for row in (0, TILE)]
    for head in range(q_ref.shape[1] // HEAD_DIM):
        cols = slice(head * HEAD_DIM, (head + 1) * HEAD_DIM)
        query = q_ref[:, cols]
        scores = []
        tops = []
        for t, (ref, row) in enumerate(tiles):
            s = lax.dot_general(
                query, ref[row : row + TILE, cols], (((1,), (1,)), ((), ())), preferred_element_type=jnp.float32
            )
            scores.append(s)
            tops.append(jnp.max(s, axis=-1, keepdims=True) + bias_ref[t])
        top = functools.reduce(jnp.maximum, tops) * LOG2_SCALE
        total = None
        blended = None
        for t, (ref, row) in enumerate(tiles):
            probs = jnp.exp2(scores[t] * LOG2_SCALE + (bias_ref[t] - top))
            row_sum = jnp.sum(probs, axis=-1, keepdims=True)
            part = jnp.dot(
                probs.astype(jnp.bfloat16),
                ref[2 * TILE + row : 3 * TILE + row, cols],
                preferred_element_type=jnp.float32,
            )
            total = row_sum if total is None else total + row_sum
            blended = part if blended is None else blended + part
        attn = (blended / total).astype(jnp.bfloat16)
        out_ref[:, cols] = (res_ref[:, cols].astype(jnp.float32) + attn.astype(jnp.float32)).astype(
            jnp.bfloat16
        )


def attend(bias, queries, residual, both, mine, theirs, first, near, heads):
    wide = 2 * HEAD_DIM
    tall = lambda rows, at: pl.BlockSpec((rows, wide), lambda i: (0, at // 2 + i))
    return pl.pallas_call(
        attend_kernel,
        out_shape=jax.ShapeDtypeStruct((TILE, heads * HEAD_DIM), jnp.bfloat16),
        grid=(heads // 2,),
        in_specs=[pl.BlockSpec(memory_space=pltpu.SMEM)] + [tall(TILE, first)] * 2 + [tall(4 * TILE, near)] * 3,
        out_specs=tall(TILE, 0),
        compiler_params=pltpu.CompilerParams(vmem_limit_bytes=VMEM_BYTES),
        cost_estimate=LIGHT,
        name="attend",
    )(bias, queries, residual, both, mine, theirs)


def gelu(x):
    return 0.5 * x * (1.0 + jnp.tanh(math.sqrt(2.0 / math.pi) * (x + 0.044715 * (x * x * x))))


def scaled_features(hid, groups, first, scale_ref, held_ref):
    square = None
    at = 0
    for half, group in zip((hid, 1 - hid), groups):
        feature = first
        for ref in group:
            width = ref.shape[1]
            gain = 1.0 + scale_ref[:, pl.ds(pl.multiple_of(half * HALF + feature, 128), width)]
            wide = ref[...].astype(jnp.float32)
            held_ref[:, at : at + width] = (wide * gain).astype(jnp.bfloat16)
            part = jnp.sum(wide * wide, axis=-1, keepdims=True)
            square = part if square is None else square + part
            feature += width
            at += width
    return square


def project_in_kernel(counts, blocks, first, has_earlier, is_last, hid_ref, *refs):
    own, other = refs[: counts[0]], refs[counts[0] : sum(counts)]
    scale_ref, *refs = refs[sum(counts) :]
    weights, refs = refs[: 2 * blocks], list(refs[2 * blocks :])
    acc_ref, earlier_square_ref = (refs.pop(0), refs.pop(0)) if has_earlier else (None, None)
    out_ref = refs.pop(0)
    square_ref, held_ref = refs

    @pl.when(pl.program_id(0) == 0)
    def _():
        square = scaled_features(hid_ref[0], (own, other), first, scale_ref, held_ref)
        square_ref[...] = square + earlier_square_ref[...] if has_earlier else square

    rows = weights[0].shape[0]
    inner = acc_ref[...] if has_earlier else None
    for i, w_ref in enumerate(weights):
        part = jnp.dot(held_ref[:, i * rows : (i + 1) * rows], w_ref[...], preferred_element_type=jnp.float32)
        inner = part if inner is None else inner + part
    if is_last:
        factor = lax.rsqrt(square_ref[...] * (1.0 / FEAT) + 1e-6)
        out_ref[...] = gelu(inner * factor).astype(jnp.bfloat16)
    else:
        out_ref[...] = inner


def project_in(hid, own, other, first, rows, mod_scale, w_in, earlier=None, is_last=False):
    cols = 512
    depth = sum(v.shape[1] for v in own)
    blocks = depth // rows
    assert first % rows == 0 and depth % rows == 0 and HALF % rows == 0
    whole = lambda v: pl.BlockSpec(v.shape, lambda i, h: (0, 0))
    column = pl.BlockSpec((TILE, cols), lambda i, h: (0, i))
    one = jax.ShapeDtypeStruct((TILE, 1), jnp.float32)
    scale = mod_scale.reshape(1, FEAT)

    def block(half, i):
        at = first // rows + i
        return pl.BlockSpec((rows, cols), lambda j, h: ((h[0] if half == 0 else 1 - h[0]) * (HALF // rows) + at, j))

    in_specs = [whole(v) for v in own + other] + [whole(scale)]
    in_specs += [block(half, i) for half in (0, 1) for i in range(blocks)]
    operands = [*own, *other, scale] + [w_in] * (2 * blocks)
    scratch = [pltpu.VMEM((TILE, 2 * depth), jnp.bfloat16)]
    if earlier is not None:
        in_specs += [column, whole(one)]
        operands += earlier
    if is_last:
        out_shape, out_specs = jax.ShapeDtypeStruct((TILE, UNITS), jnp.bfloat16), column
        scratch.insert(0, pltpu.VMEM((TILE, 1), jnp.float32))
    else:
        out_shape = (jax.ShapeDtypeStruct((TILE, UNITS), jnp.float32), one)
        out_specs = (column, whole(one))
    return pl.pallas_call(
        functools.partial(project_in_kernel, (len(own), len(other)), blocks, first, earlier is not None, is_last),
        out_shape=out_shape,
        grid_spec=pltpu.PrefetchScalarGridSpec(
            num_scalar_prefetch=1,
            grid=(UNITS // cols,),
            in_specs=in_specs,
            out_specs=out_specs,
            scratch_shapes=scratch,
        ),
        compiler_params=pltpu.CompilerParams(vmem_limit_bytes=VMEM_BYTES),
        cost_estimate=LIGHT,
        name="project_in",
    )(hid, *operands)


def project_out_kernel(part_ref, hidden_ref, w_ref, out_ref):
    out_ref[...] = lax.dot_general(
        hidden_ref[...], w_ref[...], (((1,), (1,)), ((), ())), preferred_element_type=jnp.float32
    ).astype(out_ref.dtype)


def project_out(part, hidden, w_rows, dtype):
    cols = 384
    return pl.pallas_call(
        project_out_kernel,
        out_shape=jax.ShapeDtypeStruct((TILE, QUARTER), dtype),
        grid_spec=pltpu.PrefetchScalarGridSpec(
            num_scalar_prefetch=1,
            grid=(QUARTER // cols,),
            in_specs=[
                pl.BlockSpec((TILE, UNITS), lambda i, p: (0, 0)),
                pl.BlockSpec((cols, UNITS), lambda i, p: (p[0] * (QUARTER // cols) + i, 0)),
            ],
            out_specs=pl.BlockSpec((TILE, cols), lambda i, p: (0, i)),
        ),
        compiler_params=pltpu.CompilerParams(vmem_limit_bytes=VMEM_BYTES),
        cost_estimate=LIGHT,
        name="project_out",
    )(part, hidden, w_rows)


def finish_kernel(chunk_count, core_ref, *refs):
    combined = refs[:chunk_count]
    kept_there, kept_here, received_here, received_there, gate_ref, out_ref = refs[chunk_count:]

    def write(core):
        at = 0
        for ref in combined:
            for left in range(0, ref.shape[1], 256):
                cols = slice(at + left, at + left + 256)
                near = slice(cols.start % QUARTER, cols.start % QUARTER + 256)
                if cols.start // QUARTER == core:
                    mlp = kept_there[:, near].astype(jnp.float32) + received_here[:, near].astype(jnp.float32)
                else:
                    mlp = kept_here[:, near] + received_there[:, near].astype(jnp.float32)
                wide = ref[:, left : left + 256].astype(jnp.float32)
                out_ref[:, cols] = (wide + gate_ref[:, cols] * mlp).astype(jnp.bfloat16)
            at += ref.shape[1]

    for core in (0, 1):
        pl.when(core_ref[0] == core)(functools.partial(write, core))


def finish(core, combined, kept_there, kept_here, received_here, received_there, gate):
    vmem = pl.BlockSpec(memory_space=pltpu.VMEM)
    return pl.pallas_call(
        functools.partial(finish_kernel, len(combined)),
        out_shape=jax.ShapeDtypeStruct((TILE, HALF), jnp.bfloat16),
        in_specs=[pl.BlockSpec(memory_space=pltpu.SMEM)] + [vmem] * (len(combined) + 5),
        out_specs=vmem,
        compiler_params=pltpu.CompilerParams(vmem_limit_bytes=VMEM_BYTES),
        cost_estimate=LIGHT,
        name="finish",
    )(core, *combined, kept_there, kept_here, received_here, received_there, gate)


def on_device(
    queries, keys, values, residual, w_in, w_out, mod_scale, mod_gate, slot_tiles, key_tiles
):
    seq = lax.axis_index("seq")
    hid = lax.axis_index("hid")
    core = seq % 2
    y = seq // 2 % 4
    z = seq // 8 % 4
    x_lo = seq // 32

    side = 1 - 2 * core
    slots = seq + side * jnp.array([0, 1, -2, -1, 3, 2], jnp.int32)
    inside = (slots >= 0) & (slots < slot_tiles.shape[0])
    tiles = slot_tiles[jnp.clip(slots, 0, slot_tiles.shape[0] - 1)]
    listed = jnp.any(key_tiles[slot_tiles[seq]][:, None] == tiles[None, :], axis=0)
    bias = jnp.where(listed & inside, 0.0, -jnp.inf).astype(jnp.float32)

    counts = FRAME_CHUNKS
    starts = [sum(counts[:i]) for i in range(len(counts))]
    swap = lambda v: moved(v, to_partner_core)
    join = lambda *v: jnp.concatenate(v, axis=0)
    hid_1 = hid.reshape(1)
    mine, own, others, theirs, both = [], [], [], [], []

    def pack(i):
        cols = slice(starts[i] * HEAD_DIM, (starts[i] + counts[i]) * HEAD_DIM)
        return join(keys[:, cols], values[:, cols])

    def send_frame(here, there):
        both.append(join(here[:TILE], there[:TILE], here[TILE:], there[TILE:]))
        mine.append(moved(both[-1], to_next_frame))
        return both[-1]

    def attend_heads(i, near, heads, *earlier):
        part = attend(
            after(bias, *earlier),
            queries,
            residual,
            both[i],
            mine[i],
            theirs[i],
            starts[i] + near,
            near,
            heads,
        )
        own.append(part)
        others.append(moved(part, to_other_hid))
        return part

    own_is_other_half = x_lo == 1 - hid
    gives_other_half = (core == 0) == (z < 2)
    same = [[32 * x + 2 * i + c for i in range(16)] for x in (0, 1) for c in (0, 1)]
    piece = w_out.T
    piece_x = moved(piece, along_x)
    pack_0 = after(pack(0), piece)
    other_0 = swap(pack_0)
    piece_x = after(piece_x, pack_0)
    w_hold = jnp.where(own_is_other_half == gives_other_half, piece, piece_x)
    w_pass = jnp.where(own_is_other_half == gives_other_half, piece_x, piece)
    w_take = swap(w_pass)
    done = send_frame(pack_0, after(other_0, w_pass))
    w_take = after(w_take, done)
    w_chip = join(jnp.where(core == 0, w_hold, w_take), jnp.where(core == 0, w_take, w_hold))
    w_rows = lax.all_gather(w_chip, "seq", axis=0, tiled=True, axis_index_groups=same)
    pack_1 = after(pack(1), w_chip)
    other_1 = swap(pack_1)
    done = send_frame(pack_1, other_1)
    mine[0] = after(mine[0], done)
    theirs.append(swap(mine[0]))
    done = attend_heads(0, 0, 4)
    mine[1] = after(mine[1], done, others[0])
    theirs.append(swap(mine[1]))
    done = attend_heads(1, 0, 4)
    done = attend_heads(1, 4, 4, done)
    earlier = project_in(after(hid_1, done), own[:2], others[:2], 0, 512, mod_scale, w_in)
    hidden = project_in(hid_1, own[2:], others[2:], 1024, 512, mod_scale, w_in, earlier, is_last=True)
    hidden_there = swap(hidden)
    core_1 = core.reshape(1)
    sent_here = project_out(core_1, hidden, w_rows, jnp.bfloat16)
    received_here = moved(sent_here, to_other_hid)
    hidden_there = after(hidden_there, sent_here)
    sent_there = project_out(core_1, hidden_there, w_rows, jnp.bfloat16)
    received_there = moved(sent_there, to_other_hid_crossed)
    kept_there = project_out(after(1 - core_1, sent_there), hidden_there, w_rows, jnp.bfloat16)
    kept_here = project_out(after(1 - core_1, kept_there), hidden, w_rows, jnp.float32)
    kept_there = jnp.concatenate((swap(kept_there[:, :384]), swap(kept_there[:, 384:])), axis=1)
    gate = lax.dynamic_slice_in_dim(mod_gate, hid * HALF, HALF).reshape(1, HALF)
    return finish(core_1, own, kept_there, kept_here, received_here, received_there, gate)


def solution(mesh):
    placed = (
        P("seq", "hid"),
        P("seq", "hid"),
        P("seq", "hid"),
        P("seq", "hid"),
        P(None, "hid"),
        P("hid", "seq"),
        P(),
        P(),
        P(),
        P(),
    )
    return jax.shard_map(
        on_device, mesh=mesh, in_specs=placed, out_specs=P("seq", "hid"), check_vma=False
    )
```

```python
import functools
import math

import jax
import jax.numpy as jnp
from jax import lax
from jax.experimental import pallas as pl
from jax.experimental.pallas import tpu as pltpu
from jax.sharding import PartitionSpec as P

HEAD_DIM = 128
TILE = 384
FEAT = 3072
HALF = 1536
UNITS = 3072
PIECE = 48
BLOCK = 384
QUARTER = 768
FRAME_CHUNKS = (8, 4)
LOG2_SCALE = math.log2(math.e) / math.sqrt(HEAD_DIM)
AXES = ("seq", "hid")
VMEM_BYTES = 56 << 20
SMALL_VMEM_BYTES = 24 << 20
LIGHT = pl.CostEstimate(flops=1, bytes_accessed=1, transcendentals=0)


def place(device):
    hid = device % 2
    seq = device // 2
    return seq // 32, seq // 8 % 4, seq // 2 % 4, seq % 2, hid


def device_at(x_lo, z, y, core, hid):
    return (((x_lo * 4 + z % 4) * 4 + y % 4) * 2 + core) * 2 + hid


def moved(value, target):
    pairs = []
    for device in range(128):
        there = target(*place(device))
        if there is not None:
            pairs.append((device, there))
    return lax.ppermute(value, AXES, pairs)


def after(value, *others):
    return lax.optimization_barrier((value, *others))[0]


def to_partner_core(x_lo, z, y, core, hid):
    return device_at(x_lo, z, y, 1 - core, hid)


def to_next_frame(x_lo, z, y, core, hid):
    chip = (x_lo * 4 + z) * 4 + y + (1 if core == 0 else -1)
    if not 0 <= chip < 32:
        return None
    return (chip * 2 + core) * 2 + hid


def along_y(x_lo, z, y, core, hid):
    return device_at(x_lo, z, y + (1 if core == 0 else -1), core, hid)


def along_z(x_lo, z, y, core, hid):
    return device_at(x_lo, z + (1 if core == 0 else -1), y, core, hid)


def along_x(x_lo, z, y, core, hid):
    return device_at(1 - x_lo, z, y, core, hid)


def to_other_hid(x_lo, z, y, core, hid):
    return device_at(x_lo, z, y, core, 1 - hid)


def to_other_hid_crossed(x_lo, z, y, core, hid):
    return device_at(x_lo, z, y, 1 - core, 1 - hid)


def attend_kernel(bias_ref, q_ref, res_ref, *refs):
    pairs, out_ref = refs[:3], refs[3]
    tiles = [(ref, row) for ref in pairs for row in (0, TILE)]
    for head in range(q_ref.shape[1] // HEAD_DIM):
        cols = slice(head * HEAD_DIM, (head + 1) * HEAD_DIM)
        query = q_ref[:, cols]
        scores = []
        tops = []
        for t, (ref, row) in enumerate(tiles):
            s = lax.dot_general(
                query, ref[row : row + TILE, cols], (((1,), (1,)), ((), ())), preferred_element_type=jnp.float32
            )
            scores.append(s)
            tops.append(jnp.max(s, axis=-1, keepdims=True) + bias_ref[t])
        top = functools.reduce(jnp.maximum, tops) * LOG2_SCALE
        total = None
        blended = None
        for t, (ref, row) in enumerate(tiles):
            probs = jnp.exp2(scores[t] * LOG2_SCALE + (bias_ref[t] - top))
            row_sum = jnp.sum(probs, axis=-1, keepdims=True)
            part = jnp.dot(
                probs.astype(jnp.bfloat16),
                ref[2 * TILE + row : 3 * TILE + row, cols],
                preferred_element_type=jnp.float32,
            )
            total = row_sum if total is None else total + row_sum
            blended = part if blended is None else blended + part
        attn = (blended / total).astype(jnp.bfloat16)
        out_ref[:, cols] = (res_ref[:, cols].astype(jnp.float32) + attn.astype(jnp.float32)).astype(
            jnp.bfloat16
        )


def attend(bias, queries, residual, both, mine, theirs, first, near, heads):
    wide = 2 * HEAD_DIM
    tall = lambda rows, at: pl.BlockSpec((rows, wide), lambda i: (0, at // 2 + i))
    return pl.pallas_call(
        attend_kernel,
        out_shape=jax.ShapeDtypeStruct((TILE, heads * HEAD_DIM), jnp.bfloat16),
        grid=(heads // 2,),
        in_specs=[pl.BlockSpec(memory_space=pltpu.SMEM)] + [tall(TILE, first)] * 2 + [tall(4 * TILE, near)] * 3,
        out_specs=tall(TILE, 0),
        compiler_params=pltpu.CompilerParams(vmem_limit_bytes=SMALL_VMEM_BYTES),
        cost_estimate=LIGHT,
        name="attend",
    )(bias, queries, residual, both, mine, theirs)


def gelu(x):
    return 0.5 * x * (1.0 + jnp.tanh(math.sqrt(2.0 / math.pi) * (x + 0.044715 * (x * x * x))))


def scaled_features(hid, groups, first, scale_ref, held_ref):
    square = None
    at = 0
    for half, group in zip((hid, 1 - hid), groups):
        feature = first
        for ref in group:
            width = ref.shape[1]
            gain = 1.0 + scale_ref[:, pl.ds(pl.multiple_of(half * HALF + feature, 128), width)]
            wide = ref[...].astype(jnp.float32)
            held_ref[:, at : at + width] = (wide * gain).astype(jnp.bfloat16)
            part = jnp.sum(wide * wide, axis=-1, keepdims=True)
            square = part if square is None else square + part
            feature += width
            at += width
    return square


def project_in_kernel(counts, blocks, first, has_earlier, is_last, hid_ref, *refs):
    own, other = refs[: counts[0]], refs[counts[0] : sum(counts)]
    scale_ref, *refs = refs[sum(counts) :]
    weights, refs = refs[: 2 * blocks], list(refs[2 * blocks :])
    acc_ref, earlier_square_ref = (refs.pop(0), refs.pop(0)) if has_earlier else (None, None)
    out_ref = refs.pop(0)
    square_ref, held_ref = refs

    @pl.when(pl.program_id(0) == 0)
    def _():
        square = scaled_features(hid_ref[0], (own, other), first, scale_ref, held_ref)
        square_ref[...] = square + earlier_square_ref[...] if has_earlier else square

    rows = weights[0].shape[0]
    inner = acc_ref[...] if has_earlier else None
    for i, w_ref in enumerate(weights):
        part = jnp.dot(held_ref[:, i * rows : (i + 1) * rows], w_ref[...], preferred_element_type=jnp.float32)
        inner = part if inner is None else inner + part
    if is_last:
        factor = lax.rsqrt(square_ref[...] * (1.0 / FEAT) + 1e-6)
        out_ref[...] = gelu(inner * factor).astype(jnp.bfloat16)
    else:
        out_ref[...] = inner


def project_in(hid, own, other, first, rows, mod_scale, w_in, earlier=None, is_last=False):
    cols = 512
    depth = sum(v.shape[1] for v in own)
    blocks = depth // rows
    assert first % rows == 0 and depth % rows == 0 and HALF % rows == 0
    whole = lambda v: pl.BlockSpec(v.shape, lambda i, h: (0, 0))
    column = pl.BlockSpec((TILE, cols), lambda i, h: (0, i))
    one = jax.ShapeDtypeStruct((TILE, 1), jnp.float32)
    scale = mod_scale.reshape(1, FEAT)

    def block(half, i):
        at = first // rows + i
        return pl.BlockSpec((rows, cols), lambda j, h: ((h[0] if half == 0 else 1 - h[0]) * (HALF // rows) + at, j))

    in_specs = [whole(v) for v in own + other] + [whole(scale)]
    in_specs += [block(half, i) for half in (0, 1) for i in range(blocks)]
    operands = [*own, *other, scale] + [w_in] * (2 * blocks)
    scratch = [pltpu.VMEM((TILE, 2 * depth), jnp.bfloat16)]
    if earlier is not None:
        in_specs += [column, whole(one)]
        operands += earlier
    if is_last:
        out_shape, out_specs = jax.ShapeDtypeStruct((TILE, UNITS), jnp.bfloat16), column
        scratch.insert(0, pltpu.VMEM((TILE, 1), jnp.float32))
    else:
        out_shape = (jax.ShapeDtypeStruct((TILE, UNITS), jnp.float32), one)
        out_specs = (column, whole(one))
    return pl.pallas_call(
        functools.partial(project_in_kernel, (len(own), len(other)), blocks, first, earlier is not None, is_last),
        out_shape=out_shape,
        grid_spec=pltpu.PrefetchScalarGridSpec(
            num_scalar_prefetch=1,
            grid=(UNITS // cols,),
            in_specs=in_specs,
            out_specs=out_specs,
            scratch_shapes=scratch,
        ),
        compiler_params=pltpu.CompilerParams(vmem_limit_bytes=VMEM_BYTES),
        cost_estimate=LIGHT,
        name="project_in",
    )(hid, *operands)


def project_out_kernel(part_ref, hidden_ref, w_ref, out_ref):
    out_ref[...] = lax.dot_general(
        hidden_ref[...], w_ref[...], (((1,), (1,)), ((), ())), preferred_element_type=jnp.float32
    ).astype(out_ref.dtype)


def project_out(part, hidden, w_rows, dtype):
    cols = 256
    return pl.pallas_call(
        project_out_kernel,
        out_shape=jax.ShapeDtypeStruct((TILE, QUARTER), dtype),
        grid_spec=pltpu.PrefetchScalarGridSpec(
            num_scalar_prefetch=1,
            grid=(QUARTER // cols,),
            in_specs=[
                pl.BlockSpec((TILE, UNITS), lambda i, p: (0, 0)),
                pl.BlockSpec((cols, UNITS), lambda i, p: (p[0] * (QUARTER // cols) + i, 0)),
            ],
            out_specs=pl.BlockSpec((TILE, cols), lambda i, p: (0, i)),
        ),
        compiler_params=pltpu.CompilerParams(vmem_limit_bytes=VMEM_BYTES),
        cost_estimate=LIGHT,
        name="project_out",
    )(part, hidden, w_rows)


def finish_kernel(chunk_count, core_ref, *refs):
    combined = refs[:chunk_count]
    kept_there, kept_here, received_here, received_there, gate_ref, out_ref = refs[chunk_count:]

    def write(core):
        at = 0
        for ref in combined:
            for left in range(0, ref.shape[1], 256):
                cols = slice(at + left, at + left + 256)
                near = slice(cols.start % QUARTER, cols.start % QUARTER + 256)
                if cols.start // QUARTER == core:
                    mlp = kept_there[:, near].astype(jnp.float32) + received_here[:, near].astype(jnp.float32)
                else:
                    mlp = kept_here[:, near] + received_there[:, near].astype(jnp.float32)
                wide = ref[:, left : left + 256].astype(jnp.float32)
                out_ref[:, cols] = (wide + gate_ref[:, cols] * mlp).astype(jnp.bfloat16)
            at += ref.shape[1]

    for core in (0, 1):
        pl.when(core_ref[0] == core)(functools.partial(write, core))


def finish(core, combined, kept_there, kept_here, received_here, received_there, gate):
    vmem = pl.BlockSpec(memory_space=pltpu.VMEM)
    return pl.pallas_call(
        functools.partial(finish_kernel, len(combined)),
        out_shape=jax.ShapeDtypeStruct((TILE, HALF), jnp.bfloat16),
        in_specs=[pl.BlockSpec(memory_space=pltpu.SMEM)] + [vmem] * (len(combined) + 5),
        out_specs=vmem,
        compiler_params=pltpu.CompilerParams(vmem_limit_bytes=SMALL_VMEM_BYTES),
        cost_estimate=LIGHT,
        name="finish",
    )(core, *combined, kept_there, kept_here, received_here, received_there, gate)


def on_device(
    queries, keys, values, residual, w_in, w_out, mod_scale, mod_gate, slot_tiles, key_tiles
):
    seq = lax.axis_index("seq")
    hid = lax.axis_index("hid")
    core = seq % 2
    y = seq // 2 % 4
    z = seq // 8 % 4
    x_lo = seq // 32

    side = 1 - 2 * core
    slots = seq + side * jnp.array([0, 1, -2, -1, 3, 2], jnp.int32)
    inside = (slots >= 0) & (slots < slot_tiles.shape[0])
    tiles = slot_tiles[jnp.clip(slots, 0, slot_tiles.shape[0] - 1)]
    listed = jnp.any(key_tiles[slot_tiles[seq]][:, None] == tiles[None, :], axis=0)
    bias = jnp.where(listed & inside, 0.0, -jnp.inf).astype(jnp.float32)

    counts = FRAME_CHUNKS
    starts = [sum(counts[:i]) for i in range(len(counts))]
    swap = lambda v: moved(v, to_partner_core)
    join = lambda *v: jnp.concatenate(v, axis=0)
    hid_1 = hid.reshape(1)
    mine, own, others, theirs, both = [], [], [], [], []

    def pack(i):
        cols = slice(starts[i] * HEAD_DIM, (starts[i] + counts[i]) * HEAD_DIM)
        return join(keys[:, cols], values[:, cols])

    def send_frame(here, there):
        both.append(join(here[:TILE], there[:TILE], here[TILE:], there[TILE:]))
        mine.append(moved(both[-1], to_next_frame))
        return both[-1]

    def attend_heads(i, near, heads, *earlier):
        part = attend(
            after(bias, *earlier),
            queries,
            residual,
            both[i],
            mine[i],
            theirs[i],
            starts[i] + near,
            near,
            heads,
        )
        own.append(part)
        others.append(moved(part, to_other_hid))
        return part

    own_is_other_half = x_lo == 1 - hid
    gives_other_half = (core == 0) == (z < 2)
    same = [[32 * x + 2 * i + c for i in range(16)] for x in (0, 1) for c in (0, 1)]
    piece = w_out.T
    piece_x = moved(piece, along_x)
    pack_0 = after(pack(0), piece)
    other_0 = swap(pack_0)
    done = send_frame(pack_0, other_0)
    piece_x = after(piece_x, done)
    w_hold = jnp.where(own_is_other_half == gives_other_half, piece, piece_x)
    w_pass = jnp.where(own_is_other_half == gives_other_half, piece_x, piece)
    w_take = swap(w_pass)
    w_chip = join(jnp.where(core == 0, w_hold, w_take), jnp.where(core == 0, w_take, w_hold))
    w_rows = lax.all_gather(w_chip, "seq", axis=0, tiled=True, axis_index_groups=same)
    pack_1 = after(pack(1), w_chip)
    other_1 = swap(pack_1)
    done = send_frame(pack_1, other_1)
    mine[0] = after(mine[0], done)
    theirs.append(swap(mine[0]))
    done = attend_heads(0, 0, 4)
    done = attend_heads(0, 4, 4, done)
    mine[1] = after(mine[1], done)
    theirs.append(swap(mine[1]))
    done = attend_heads(1, 0, 4)
    hidden = project_in(after(hid_1, done), own, others, 0, HALF, mod_scale, w_in, is_last=True)
    hidden_there = swap(hidden)
    core_1 = core.reshape(1)
    sent_here = project_out(core_1, hidden, w_rows, jnp.bfloat16)
    received_here = moved(sent_here, to_other_hid)
    hidden_there = after(hidden_there, sent_here)
    sent_there = project_out(core_1, hidden_there, w_rows, jnp.bfloat16)
    received_there = moved(sent_there, to_other_hid_crossed)
    kept_there = project_out(after(1 - core_1, sent_there), hidden_there, w_rows, jnp.bfloat16)
    kept_here = project_out(after(1 - core_1, kept_there), hidden, w_rows, jnp.float32)
    kept_there = jnp.concatenate((swap(kept_there[:, :384]), swap(kept_there[:, 384:])), axis=1)
    gate = lax.dynamic_slice_in_dim(mod_gate, hid * HALF, HALF).reshape(1, HALF)
    return finish(core_1, own, kept_there, kept_here, received_here, received_there, gate)


def solution(mesh):
    placed = (
        P("seq", "hid"),
        P("seq", "hid"),
        P("seq", "hid"),
        P("seq", "hid"),
        P(None, "hid"),
        P("hid", "seq"),
        P(),
        P(),
        P(),
        P(),
    )
    return jax.shard_map(
        on_device, mesh=mesh, in_specs=placed, out_specs=P("seq", "hid"), check_vma=False
    )
```

```python
import functools
import math

import jax
import jax.numpy as jnp
from jax import lax
from jax.experimental import pallas as pl
from jax.experimental.pallas import tpu as pltpu
from jax.sharding import PartitionSpec as P

HEAD_DIM = 128
TILE = 384
FEAT = 3072
HALF = 1536
UNITS = 3072
PIECE = 48
BLOCK = 384
QUARTER = 768
FRAME_CHUNKS = (8, 4)
LOG2_SCALE = math.log2(math.e) / math.sqrt(HEAD_DIM)
AXES = ("seq", "hid")
VMEM_BYTES = 56 << 20
SMALL_VMEM_BYTES = 24 << 20
LIGHT = pl.CostEstimate(flops=1, bytes_accessed=1, transcendentals=0)


def place(device):
    hid = device % 2
    seq = device // 2
    return seq // 32, seq // 8 % 4, seq // 2 % 4, seq % 2, hid


def device_at(x_lo, z, y, core, hid):
    return (((x_lo * 4 + z % 4) * 4 + y % 4) * 2 + core) * 2 + hid


def moved(value, target):
    pairs = []
    for device in range(128):
        there = target(*place(device))
        if there is not None:
            pairs.append((device, there))
    return lax.ppermute(value, AXES, pairs)


def after(value, *others):
    return lax.optimization_barrier((value, *others))[0]


def to_partner_core(x_lo, z, y, core, hid):
    return device_at(x_lo, z, y, 1 - core, hid)


def to_next_frame(x_lo, z, y, core, hid):
    chip = (x_lo * 4 + z) * 4 + y + (1 if core == 0 else -1)
    if not 0 <= chip < 32:
        return None
    return (chip * 2 + core) * 2 + hid


def along_y(x_lo, z, y, core, hid):
    return device_at(x_lo, z, y + (1 if core == 0 else -1), core, hid)


def along_z(x_lo, z, y, core, hid):
    return device_at(x_lo, z + (1 if core == 0 else -1), y, core, hid)


def along_x(x_lo, z, y, core, hid):
    return device_at(1 - x_lo, z, y, core, hid)


def to_other_hid(x_lo, z, y, core, hid):
    return device_at(x_lo, z, y, core, 1 - hid)


def to_other_hid_crossed(x_lo, z, y, core, hid):
    return device_at(x_lo, z, y, 1 - core, 1 - hid)


def attend_kernel(bias_ref, q_ref, res_ref, *refs):
    pairs, out_ref = refs[:3], refs[3]
    tiles = [(ref, row) for ref in pairs for row in (0, TILE)]
    for head in range(q_ref.shape[1] // HEAD_DIM):
        cols = slice(head * HEAD_DIM, (head + 1) * HEAD_DIM)
        query = q_ref[:, cols]
        scores = []
        tops = []
        for t, (ref, row) in enumerate(tiles):
            s = lax.dot_general(
                query, ref[row : row + TILE, cols], (((1,), (1,)), ((), ())), preferred_element_type=jnp.float32
            )
            scores.append(s)
            tops.append(jnp.max(s, axis=-1, keepdims=True) + bias_ref[t])
        top = functools.reduce(jnp.maximum, tops) * LOG2_SCALE
        total = None
        blended = None
        for t, (ref, row) in enumerate(tiles):
            probs = jnp.exp2(scores[t] * LOG2_SCALE + (bias_ref[t] - top))
            row_sum = jnp.sum(probs, axis=-1, keepdims=True)
            part = jnp.dot(
                probs.astype(jnp.bfloat16),
                ref[2 * TILE + row : 3 * TILE + row, cols],
                preferred_element_type=jnp.float32,
            )
            total = row_sum if total is None else total + row_sum
            blended = part if blended is None else blended + part
        attn = (blended / total).astype(jnp.bfloat16)
        out_ref[:, cols] = (res_ref[:, cols].astype(jnp.float32) + attn.astype(jnp.float32)).astype(
            jnp.bfloat16
        )


def attend(bias, queries, residual, both, mine, theirs, first, near, heads):
    wide = 2 * HEAD_DIM
    tall = lambda rows, at: pl.BlockSpec((rows, wide), lambda i: (0, at // 2 + i))
    return pl.pallas_call(
        attend_kernel,
        out_shape=jax.ShapeDtypeStruct((TILE, heads * HEAD_DIM), jnp.bfloat16),
        grid=(heads // 2,),
        in_specs=[pl.BlockSpec(memory_space=pltpu.SMEM)] + [tall(TILE, first)] * 2 + [tall(4 * TILE, near)] * 3,
        out_specs=tall(TILE, 0),
        compiler_params=pltpu.CompilerParams(vmem_limit_bytes=SMALL_VMEM_BYTES),
        cost_estimate=LIGHT,
        name="attend",
    )(bias, queries, residual, both, mine, theirs)


def gelu(x):
    return 0.5 * x * (1.0 + jnp.tanh(math.sqrt(2.0 / math.pi) * (x + 0.044715 * (x * x * x))))


def scaled_features(hid, groups, first, scale_ref, held_ref):
    square = None
    at = 0
    for half, group in zip((hid, 1 - hid), groups):
        feature = first
        for ref in group:
            width = ref.shape[1]
            gain = 1.0 + scale_ref[:, pl.ds(pl.multiple_of(half * HALF + feature, 128), width)]
            wide = ref[...].astype(jnp.float32)
            held_ref[:, at : at + width] = (wide * gain).astype(jnp.bfloat16)
            part = jnp.sum(wide * wide, axis=-1, keepdims=True)
            square = part if square is None else square + part
            feature += width
            at += width
    return square


def project_in_kernel(counts, blocks, first, has_earlier, is_last, hid_ref, *refs):
    own, other = refs[: counts[0]], refs[counts[0] : sum(counts)]
    scale_ref, *refs = refs[sum(counts) :]
    weights, refs = refs[:blocks], list(refs[blocks:])
    acc_ref, earlier_square_ref = (refs.pop(0), refs.pop(0)) if has_earlier else (None, None)
    out_ref = refs.pop(0)
    square_ref, held_ref = refs

    @pl.when(pl.program_id(0) == 0)
    def _():
        square = scaled_features(hid_ref[0], (own, other), first, scale_ref, held_ref)
        square_ref[...] = square + earlier_square_ref[...] if has_earlier else square

    rows = weights[0].shape[0]
    inner = acc_ref[...] if has_earlier else None
    for i, w_ref in enumerate(weights):
        part = jnp.dot(held_ref[:, i * rows : (i + 1) * rows], w_ref[...], preferred_element_type=jnp.float32)
        inner = part if inner is None else inner + part
    if is_last:
        factor = lax.rsqrt(square_ref[...] * (1.0 / FEAT) + 1e-6)
        out_ref[...] = gelu(inner * factor).astype(jnp.bfloat16)
    else:
        out_ref[...] = inner


def project_in(hid, own, other, first, rows, mod_scale, w_in, earlier=None, is_last=False):
    cols = 512
    depths = [sum(v.shape[1] for v in group) for group in (own, other)]
    blocks = [(half, i) for half, depth in enumerate(depths) for i in range(depth // rows)]
    assert first % rows == 0 and HALF % rows == 0 and all(depth % rows == 0 for depth in depths)
    whole = lambda v: pl.BlockSpec(v.shape, lambda i, h: (0, 0))
    column = pl.BlockSpec((TILE, cols), lambda i, h: (0, i))
    one = jax.ShapeDtypeStruct((TILE, 1), jnp.float32)
    scale = mod_scale.reshape(1, FEAT)

    def block(half, i):
        at = first // rows + i
        return pl.BlockSpec((rows, cols), lambda j, h: ((h[0] if half == 0 else 1 - h[0]) * (HALF // rows) + at, j))

    in_specs = [whole(v) for v in own + other] + [whole(scale)]
    in_specs += [block(half, i) for half, i in blocks]
    operands = [*own, *other, scale] + [w_in] * len(blocks)
    scratch = [pltpu.VMEM((TILE, sum(depths)), jnp.bfloat16)]
    if earlier is not None:
        in_specs += [column, whole(one)]
        operands += earlier
    if is_last:
        out_shape, out_specs = jax.ShapeDtypeStruct((TILE, UNITS), jnp.bfloat16), column
        scratch.insert(0, pltpu.VMEM((TILE, 1), jnp.float32))
    else:
        out_shape = (jax.ShapeDtypeStruct((TILE, UNITS), jnp.float32), one)
        out_specs = (column, whole(one))
    return pl.pallas_call(
        functools.partial(project_in_kernel, (len(own), len(other)), len(blocks), first, earlier is not None, is_last),
        out_shape=out_shape,
        grid_spec=pltpu.PrefetchScalarGridSpec(
            num_scalar_prefetch=1,
            grid=(UNITS // cols,),
            in_specs=in_specs,
            out_specs=out_specs,
            scratch_shapes=scratch,
        ),
        compiler_params=pltpu.CompilerParams(vmem_limit_bytes=VMEM_BYTES),
        cost_estimate=LIGHT,
        name="project_in",
    )(hid, *operands)


def project_out_kernel(part_ref, hidden_ref, w_ref, out_ref):
    out_ref[...] = lax.dot_general(
        hidden_ref[...], w_ref[...], (((1,), (1,)), ((), ())), preferred_element_type=jnp.float32
    ).astype(out_ref.dtype)


def project_out(part, hidden, w_rows, dtype):
    cols = 256
    return pl.pallas_call(
        project_out_kernel,
        out_shape=jax.ShapeDtypeStruct((TILE, QUARTER), dtype),
        grid_spec=pltpu.PrefetchScalarGridSpec(
            num_scalar_prefetch=1,
            grid=(QUARTER // cols,),
            in_specs=[
                pl.BlockSpec((TILE, UNITS), lambda i, p: (0, 0)),
                pl.BlockSpec((cols, UNITS), lambda i, p: (p[0] * (QUARTER // cols) + i, 0)),
            ],
            out_specs=pl.BlockSpec((TILE, cols), lambda i, p: (0, i)),
        ),
        compiler_params=pltpu.CompilerParams(vmem_limit_bytes=VMEM_BYTES),
        cost_estimate=LIGHT,
        name="project_out",
    )(part, hidden, w_rows)


def finish_kernel(chunk_count, core_ref, *refs):
    combined = refs[:chunk_count]
    kept_there, kept_here, received_here, received_there, gate_ref, out_ref = refs[chunk_count:]

    def write(core):
        at = 0
        for ref in combined:
            for left in range(0, ref.shape[1], 256):
                cols = slice(at + left, at + left + 256)
                near = slice(cols.start % QUARTER, cols.start % QUARTER + 256)
                if cols.start // QUARTER == core:
                    mlp = kept_there[:, near].astype(jnp.float32) + received_here[:, near].astype(jnp.float32)
                else:
                    mlp = kept_here[:, near] + received_there[:, near].astype(jnp.float32)
                wide = ref[:, left : left + 256].astype(jnp.float32)
                out_ref[:, cols] = (wide + gate_ref[:, cols] * mlp).astype(jnp.bfloat16)
            at += ref.shape[1]

    for core in (0, 1):
        pl.when(core_ref[0] == core)(functools.partial(write, core))


def finish(core, combined, kept_there, kept_here, received_here, received_there, gate):
    vmem = pl.BlockSpec(memory_space=pltpu.VMEM)
    return pl.pallas_call(
        functools.partial(finish_kernel, len(combined)),
        out_shape=jax.ShapeDtypeStruct((TILE, HALF), jnp.bfloat16),
        in_specs=[pl.BlockSpec(memory_space=pltpu.SMEM)] + [vmem] * (len(combined) + 5),
        out_specs=vmem,
        compiler_params=pltpu.CompilerParams(vmem_limit_bytes=SMALL_VMEM_BYTES),
        cost_estimate=LIGHT,
        name="finish",
    )(core, *combined, kept_there, kept_here, received_here, received_there, gate)


def on_device(
    queries, keys, values, residual, w_in, w_out, mod_scale, mod_gate, slot_tiles, key_tiles
):
    seq = lax.axis_index("seq")
    hid = lax.axis_index("hid")
    core = seq % 2
    y = seq // 2 % 4
    z = seq // 8 % 4
    x_lo = seq // 32

    side = 1 - 2 * core
    slots = seq + side * jnp.array([0, 1, -2, -1, 3, 2], jnp.int32)
    inside = (slots >= 0) & (slots < slot_tiles.shape[0])
    tiles = slot_tiles[jnp.clip(slots, 0, slot_tiles.shape[0] - 1)]
    listed = jnp.any(key_tiles[slot_tiles[seq]][:, None] == tiles[None, :], axis=0)
    bias = jnp.where(listed & inside, 0.0, -jnp.inf).astype(jnp.float32)

    counts = FRAME_CHUNKS
    starts = [sum(counts[:i]) for i in range(len(counts))]
    swap = lambda v: moved(v, to_partner_core)
    join = lambda *v: jnp.concatenate(v, axis=0)
    hid_1 = hid.reshape(1)
    mine, own, others, theirs, both = [], [], [], [], []

    def pack(i):
        cols = slice(starts[i] * HEAD_DIM, (starts[i] + counts[i]) * HEAD_DIM)
        return join(keys[:, cols], values[:, cols])

    def send_frame(here, there):
        both.append(join(here[:TILE], there[:TILE], here[TILE:], there[TILE:]))
        mine.append(moved(both[-1], to_next_frame))
        return both[-1]

    def attend_heads(i, near, heads, *earlier):
        part = attend(
            after(bias, *earlier),
            queries,
            residual,
            both[i],
            mine[i],
            theirs[i],
            starts[i] + near,
            near,
            heads,
        )
        own.append(part)
        others.append(moved(part, to_other_hid))
        return part

    own_is_other_half = x_lo == 1 - hid
    gives_other_half = (core == 0) == (z < 2)
    same = [[32 * x + 2 * i + c for i in range(16)] for x in (0, 1) for c in (0, 1)]
    piece = w_out.T
    piece_x = moved(piece, along_x)
    pack_0 = after(pack(0), piece)
    other_0 = swap(pack_0)
    piece_x = after(piece_x, pack_0)
    w_hold = jnp.where(own_is_other_half == gives_other_half, piece, piece_x)
    w_pass = jnp.where(own_is_other_half == gives_other_half, piece_x, piece)
    w_take = swap(w_pass)
    done = send_frame(pack_0, after(other_0, w_pass))
    w_take = after(w_take, done)
    w_chip = join(jnp.where(core == 0, w_hold, w_take), jnp.where(core == 0, w_take, w_hold))
    w_rows = lax.all_gather(w_chip, "seq", axis=0, tiled=True, axis_index_groups=same)
    pack_1 = after(pack(1), w_chip)
    other_1 = swap(pack_1)
    done = send_frame(pack_1, other_1)
    mine[0] = after(mine[0], done)
    theirs.append(swap(mine[0]))
    done = attend_heads(0, 0, 4)
    done = attend_heads(0, 4, 4, done)
    mine[1] = after(mine[1], done)
    theirs.append(swap(mine[1]))
    done = attend_heads(1, 0, 4)
    earlier = project_in(after(hid_1, done), own, [], 0, HALF, mod_scale, w_in)
    hidden = project_in(hid_1, [], others, 0, HALF, mod_scale, w_in, earlier, is_last=True)
    hidden_there = swap(hidden)
    core_1 = core.reshape(1)
    sent_here = project_out(core_1, hidden, w_rows, jnp.bfloat16)
    received_here = moved(sent_here, to_other_hid)
    hidden_there = after(hidden_there, sent_here)
    sent_there = project_out(core_1, hidden_there, w_rows, jnp.bfloat16)
    received_there = moved(sent_there, to_other_hid_crossed)
    kept_there = project_out(after(1 - core_1, sent_there), hidden_there, w_rows, jnp.bfloat16)
    kept_here = project_out(after(1 - core_1, kept_there), hidden, w_rows, jnp.float32)
    kept_there = jnp.concatenate((swap(kept_there[:, :384]), swap(kept_there[:, 384:])), axis=1)
    gate = lax.dynamic_slice_in_dim(mod_gate, hid * HALF, HALF).reshape(1, HALF)
    return finish(core_1, own, kept_there, kept_here, received_here, received_there, gate)


def solution(mesh):
    placed = (
        P("seq", "hid"),
        P("seq", "hid"),
        P("seq", "hid"),
        P("seq", "hid"),
        P(None, "hid"),
        P("hid", "seq"),
        P(),
        P(),
        P(),
        P(),
    )
    return jax.shard_map(
        on_device, mesh=mesh, in_specs=placed, out_specs=P("seq", "hid"), check_vma=False
    )
```

```python
import functools
import math

import jax
import jax.numpy as jnp
from jax import lax
from jax.experimental import pallas as pl
from jax.experimental.pallas import tpu as pltpu
from jax.sharding import PartitionSpec as P

HEAD_DIM = 128
TILE = 384
FEAT = 3072
HALF = 1536
UNITS = 3072
PIECE = 48
BLOCK = 384
QUARTER = 768
FRAME_CHUNKS = (8, 4)
LOG2_SCALE = math.log2(math.e) / math.sqrt(HEAD_DIM)
AXES = ("seq", "hid")
VMEM_BYTES = 56 << 20
SMALL_VMEM_BYTES = 24 << 20
LIGHT = pl.CostEstimate(flops=1, bytes_accessed=1, transcendentals=0)


def place(device):
    hid = device % 2
    seq = device // 2
    return seq // 32, seq // 8 % 4, seq // 2 % 4, seq % 2, hid


def device_at(x_lo, z, y, core, hid):
    return (((x_lo * 4 + z % 4) * 4 + y % 4) * 2 + core) * 2 + hid


def moved(value, target):
    pairs = []
    for device in range(128):
        there = target(*place(device))
        if there is not None:
            pairs.append((device, there))
    return lax.ppermute(value, AXES, pairs)


def after(value, *others):
    return lax.optimization_barrier((value, *others))[0]


def to_partner_core(x_lo, z, y, core, hid):
    return device_at(x_lo, z, y, 1 - core, hid)


def to_next_frame(x_lo, z, y, core, hid):
    chip = (x_lo * 4 + z) * 4 + y + (1 if core == 0 else -1)
    if not 0 <= chip < 32:
        return None
    return (chip * 2 + core) * 2 + hid


def along_y(x_lo, z, y, core, hid):
    return device_at(x_lo, z, y + (1 if core == 0 else -1), core, hid)


def along_z(x_lo, z, y, core, hid):
    return device_at(x_lo, z + (1 if core == 0 else -1), y, core, hid)


def along_x(x_lo, z, y, core, hid):
    return device_at(1 - x_lo, z, y, core, hid)


def to_other_hid(x_lo, z, y, core, hid):
    return device_at(x_lo, z, y, core, 1 - hid)


def to_other_hid_crossed(x_lo, z, y, core, hid):
    return device_at(x_lo, z, y, 1 - core, 1 - hid)


def attend_kernel(bias_ref, q_ref, res_ref, *refs):
    pairs, out_ref = refs[:3], refs[3]
    tiles = [(ref, row) for ref in pairs for row in (0, TILE)]
    for head in range(q_ref.shape[1] // HEAD_DIM):
        cols = slice(head * HEAD_DIM, (head + 1) * HEAD_DIM)
        query = q_ref[:, cols]
        scores = []
        tops = []
        for t, (ref, row) in enumerate(tiles):
            s = lax.dot_general(
                query, ref[row : row + TILE, cols], (((1,), (1,)), ((), ())), preferred_element_type=jnp.float32
            )
            scores.append(s)
            tops.append(jnp.max(s, axis=-1, keepdims=True) + bias_ref[t])
        top = functools.reduce(jnp.maximum, tops) * LOG2_SCALE
        total = None
        blended = None
        for t, (ref, row) in enumerate(tiles):
            probs = jnp.exp2(scores[t] * LOG2_SCALE + (bias_ref[t] - top))
            row_sum = jnp.sum(probs, axis=-1, keepdims=True)
            part = jnp.dot(
                probs.astype(jnp.bfloat16),
                ref[2 * TILE + row : 3 * TILE + row, cols],
                preferred_element_type=jnp.float32,
            )
            total = row_sum if total is None else total + row_sum
            blended = part if blended is None else blended + part
        attn = (blended / total).astype(jnp.bfloat16)
        out_ref[:, cols] = (res_ref[:, cols].astype(jnp.float32) + attn.astype(jnp.float32)).astype(
            jnp.bfloat16
        )


def attend(bias, queries, residual, both, mine, theirs, first, near, heads):
    wide = 2 * HEAD_DIM
    tall = lambda rows, at: pl.BlockSpec((rows, wide), lambda i: (0, at // 2 + i))
    return pl.pallas_call(
        attend_kernel,
        out_shape=jax.ShapeDtypeStruct((TILE, heads * HEAD_DIM), jnp.bfloat16),
        grid=(heads // 2,),
        in_specs=[pl.BlockSpec(memory_space=pltpu.SMEM)] + [tall(TILE, first)] * 2 + [tall(4 * TILE, near)] * 3,
        out_specs=tall(TILE, 0),
        compiler_params=pltpu.CompilerParams(vmem_limit_bytes=SMALL_VMEM_BYTES),
        cost_estimate=LIGHT,
        name="attend",
    )(bias, queries, residual, both, mine, theirs)


def gelu(x):
    return 0.5 * x * (1.0 + jnp.tanh(math.sqrt(2.0 / math.pi) * (x + 0.044715 * (x * x * x))))


def scaled_features(hid, groups, first, scale_ref, held_ref):
    square = None
    at = 0
    for half, group in zip((hid, 1 - hid), groups):
        feature = first
        for ref in group:
            width = ref.shape[1]
            gain = 1.0 + scale_ref[:, pl.ds(pl.multiple_of(half * HALF + feature, 128), width)]
            wide = ref[...].astype(jnp.float32)
            held_ref[:, at : at + width] = (wide * gain).astype(jnp.bfloat16)
            part = jnp.sum(wide * wide, axis=-1, keepdims=True)
            square = part if square is None else square + part
            feature += width
            at += width
    return square


def project_in_kernel(counts, blocks, first, has_earlier, is_last, hid_ref, *refs):
    own, other = refs[: counts[0]], refs[counts[0] : sum(counts)]
    scale_ref, *refs = refs[sum(counts) :]
    weights, refs = refs[:blocks], list(refs[blocks:])
    acc_ref, earlier_square_ref = (refs.pop(0), refs.pop(0)) if has_earlier else (None, None)
    out_ref = refs.pop(0)
    square_ref, held_ref = refs

    @pl.when(pl.program_id(0) == 0)
    def _():
        square = scaled_features(hid_ref[0], (own, other), first, scale_ref, held_ref)
        square_ref[...] = square + earlier_square_ref[...] if has_earlier else square

    rows = weights[0].shape[0]
    inner = acc_ref[...] if has_earlier else None
    for i, w_ref in enumerate(weights):
        part = jnp.dot(held_ref[:, i * rows : (i + 1) * rows], w_ref[...], preferred_element_type=jnp.float32)
        inner = part if inner is None else inner + part
    if is_last:
        factor = lax.rsqrt(square_ref[...] * (1.0 / FEAT) + 1e-6)
        out_ref[...] = gelu(inner * factor).astype(jnp.bfloat16)
    else:
        out_ref[...] = inner


def project_in(hid, own, other, first, rows, mod_scale, w_in, earlier=None, is_last=False):
    cols = 512
    depths = [sum(v.shape[1] for v in group) for group in (own, other)]
    blocks = [(half, i) for half, depth in enumerate(depths) for i in range(depth // rows)]
    assert first % rows == 0 and HALF % rows == 0 and all(depth % rows == 0 for depth in depths)
    whole = lambda v: pl.BlockSpec(v.shape, lambda i, h: (0, 0))
    column = pl.BlockSpec((TILE, cols), lambda i, h: (0, i))
    one = jax.ShapeDtypeStruct((TILE, 1), jnp.float32)
    scale = mod_scale.reshape(1, FEAT)

    def block(half, i):
        at = first // rows + i
        return pl.BlockSpec((rows, cols), lambda j, h: ((h[0] if half == 0 else 1 - h[0]) * (HALF // rows) + at, j))

    in_specs = [whole(v) for v in own + other] + [whole(scale)]
    in_specs += [block(half, i) for half, i in blocks]
    operands = [*own, *other, scale] + [w_in] * len(blocks)
    scratch = [pltpu.VMEM((TILE, sum(depths)), jnp.bfloat16)]
    if earlier is not None:
        in_specs += [column, whole(one)]
        operands += earlier
    if is_last:
        out_shape, out_specs = jax.ShapeDtypeStruct((TILE, UNITS), jnp.bfloat16), column
        scratch.insert(0, pltpu.VMEM((TILE, 1), jnp.float32))
    else:
        out_shape = (jax.ShapeDtypeStruct((TILE, UNITS), jnp.float32), one)
        out_specs = (column, whole(one))
    return pl.pallas_call(
        functools.partial(project_in_kernel, (len(own), len(other)), len(blocks), first, earlier is not None, is_last),
        out_shape=out_shape,
        grid_spec=pltpu.PrefetchScalarGridSpec(
            num_scalar_prefetch=1,
            grid=(UNITS // cols,),
            in_specs=in_specs,
            out_specs=out_specs,
            scratch_shapes=scratch,
        ),
        compiler_params=pltpu.CompilerParams(vmem_limit_bytes=VMEM_BYTES),
        cost_estimate=LIGHT,
        name="project_in",
    )(hid, *operands)


def project_out_kernel(part_ref, hidden_ref, w_ref, out_ref, w_buf, sems):
    cols = 256
    copies = []
    for i in range(QUARTER // cols):
        row = pl.multiple_of(part_ref[0] * QUARTER + i * cols, cols)
        copies.append(pltpu.make_async_copy(w_ref.at[pl.ds(row, cols)], w_buf.at[i], sems.at[i]))
    for copy in copies:
        copy.start()
    for i, copy in enumerate(copies):
        copy.wait()
        out_ref[:, i * cols : (i + 1) * cols] = lax.dot_general(
            hidden_ref[...], w_buf[i], (((1,), (1,)), ((), ())), preferred_element_type=jnp.float32
        ).astype(out_ref.dtype)


def project_out(part, hidden, w_rows, dtype):
    vmem = pl.BlockSpec(memory_space=pltpu.VMEM)
    return pl.pallas_call(
        project_out_kernel,
        out_shape=jax.ShapeDtypeStruct((TILE, QUARTER), dtype),
        in_specs=[pl.BlockSpec(memory_space=pltpu.SMEM), vmem, pl.BlockSpec(memory_space=pl.ANY)],
        out_specs=vmem,
        scratch_shapes=[pltpu.VMEM((3, 256, UNITS), jnp.bfloat16), pltpu.SemaphoreType.DMA((3,))],
        compiler_params=pltpu.CompilerParams(vmem_limit_bytes=VMEM_BYTES),
        cost_estimate=LIGHT,
        name="project_out",
    )(part, hidden, w_rows)


def finish_kernel(chunk_count, core_ref, *refs):
    combined = refs[:chunk_count]
    kept_there, kept_here, received_here, received_there, gate_ref, out_ref = refs[chunk_count:]

    def write(core):
        at = 0
        for ref in combined:
            for left in range(0, ref.shape[1], 256):
                cols = slice(at + left, at + left + 256)
                near = slice(cols.start % QUARTER, cols.start % QUARTER + 256)
                if cols.start // QUARTER == core:
                    mlp = kept_there[:, near].astype(jnp.float32) + received_here[:, near].astype(jnp.float32)
                else:
                    mlp = kept_here[:, near] + received_there[:, near].astype(jnp.float32)
                wide = ref[:, left : left + 256].astype(jnp.float32)
                out_ref[:, cols] = (wide + gate_ref[:, cols] * mlp).astype(jnp.bfloat16)
            at += ref.shape[1]

    for core in (0, 1):
        pl.when(core_ref[0] == core)(functools.partial(write, core))


def finish(core, combined, kept_there, kept_here, received_here, received_there, gate):
    vmem = pl.BlockSpec(memory_space=pltpu.VMEM)
    return pl.pallas_call(
        functools.partial(finish_kernel, len(combined)),
        out_shape=jax.ShapeDtypeStruct((TILE, HALF), jnp.bfloat16),
        in_specs=[pl.BlockSpec(memory_space=pltpu.SMEM)] + [vmem] * (len(combined) + 5),
        out_specs=vmem,
        compiler_params=pltpu.CompilerParams(vmem_limit_bytes=SMALL_VMEM_BYTES),
        cost_estimate=LIGHT,
        name="finish",
    )(core, *combined, kept_there, kept_here, received_here, received_there, gate)


def on_device(
    queries, keys, values, residual, w_in, w_out, mod_scale, mod_gate, slot_tiles, key_tiles
):
    seq = lax.axis_index("seq")
    hid = lax.axis_index("hid")
    core = seq % 2
    y = seq // 2 % 4
    z = seq // 8 % 4
    x_lo = seq // 32

    side = 1 - 2 * core
    slots = seq + side * jnp.array([0, 1, -2, -1, 3, 2], jnp.int32)
    inside = (slots >= 0) & (slots < slot_tiles.shape[0])
    tiles = slot_tiles[jnp.clip(slots, 0, slot_tiles.shape[0] - 1)]
    listed = jnp.any(key_tiles[slot_tiles[seq]][:, None] == tiles[None, :], axis=0)
    bias = jnp.where(listed & inside, 0.0, -jnp.inf).astype(jnp.float32)

    counts = FRAME_CHUNKS
    starts = [sum(counts[:i]) for i in range(len(counts))]
    swap = lambda v: moved(v, to_partner_core)
    join = lambda *v: jnp.concatenate(v, axis=0)
    hid_1 = hid.reshape(1)
    mine, own, others, theirs, both = [], [], [], [], []

    def pack(i):
        cols = slice(starts[i] * HEAD_DIM, (starts[i] + counts[i]) * HEAD_DIM)
        return join(keys[:, cols], values[:, cols])

    def send_frame(here, there):
        both.append(join(here[:TILE], there[:TILE], here[TILE:], there[TILE:]))
        mine.append(moved(both[-1], to_next_frame))
        return both[-1]

    def attend_heads(i, near, heads, *earlier):
        part = attend(
            after(bias, *earlier),
            queries,
            residual,
            both[i],
            mine[i],
            theirs[i],
            starts[i] + near,
            near,
            heads,
        )
        own.append(part)
        others.append(moved(part, to_other_hid))
        return part

    own_is_other_half = x_lo == 1 - hid
    gives_other_half = (core == 0) == (z < 2)
    same = [[32 * x + 2 * i + c for i in range(16)] for x in (0, 1) for c in (0, 1)]
    piece = w_out.T
    piece_x = moved(piece, along_x)
    pack_0 = after(pack(0), piece)
    other_0 = swap(pack_0)
    piece_x = after(piece_x, pack_0)
    w_hold = jnp.where(own_is_other_half == gives_other_half, piece, piece_x)
    w_pass = jnp.where(own_is_other_half == gives_other_half, piece_x, piece)
    w_take = swap(w_pass)
    done = send_frame(pack_0, after(other_0, w_pass))
    w_take = after(w_take, done)
    w_chip = join(jnp.where(core == 0, w_hold, w_take), jnp.where(core == 0, w_take, w_hold))
    w_rows = lax.all_gather(w_chip, "seq", axis=0, tiled=True, axis_index_groups=same)
    pack_1 = after(pack(1), w_chip)
    other_1 = swap(pack_1)
    done = send_frame(pack_1, other_1)
    mine[0] = after(mine[0], done)
    theirs.append(swap(mine[0]))
    done = attend_heads(0, 0, 4)
    done = attend_heads(0, 4, 4, done)
    mine[1] = after(mine[1], done)
    theirs.append(swap(mine[1]))
    done = attend_heads(1, 0, 4)
    earlier = project_in(after(hid_1, done), own, [], 0, HALF, mod_scale, w_in)
    hidden = project_in(hid_1, [], others, 0, HALF, mod_scale, w_in, earlier, is_last=True)
    hidden_there = swap(hidden)
    core_1 = core.reshape(1)
    sent_here = project_out(core_1, hidden, w_rows, jnp.bfloat16)
    received_here = moved(sent_here, to_other_hid)
    hidden_there = after(hidden_there, sent_here)
    sent_there = project_out(core_1, hidden_there, w_rows, jnp.bfloat16)
    received_there = moved(sent_there, to_other_hid_crossed)
    kept_there = project_out(after(1 - core_1, sent_there), hidden_there, w_rows, jnp.bfloat16)
    kept_here = project_out(after(1 - core_1, kept_there), hidden, w_rows, jnp.float32)
    kept_there = jnp.concatenate((swap(kept_there[:, :384]), swap(kept_there[:, 384:])), axis=1)
    gate = lax.dynamic_slice_in_dim(mod_gate, hid * HALF, HALF).reshape(1, HALF)
    return finish(core_1, own, kept_there, kept_here, received_here, received_there, gate)


def solution(mesh):
    placed = (
        P("seq", "hid"),
        P("seq", "hid"),
        P("seq", "hid"),
        P("seq", "hid"),
        P(None, "hid"),
        P("hid", "seq"),
        P(),
        P(),
        P(),
        P(),
    )
    return jax.shard_map(
        on_device, mesh=mesh, in_specs=placed, out_specs=P("seq", "hid"), check_vma=False
    )
```

```python
import functools
import math

import jax
import jax.numpy as jnp
from jax import lax
from jax.experimental import pallas as pl
from jax.experimental.pallas import tpu as pltpu
from jax.sharding import PartitionSpec as P

HEAD_DIM = 128
TILE = 384
FEAT = 3072
HALF = 1536
UNITS = 3072
PIECE = 48
BLOCK = 384
QUARTER = 768
FRAME_CHUNKS = (8, 4)
LOG2_SCALE = math.log2(math.e) / math.sqrt(HEAD_DIM)
AXES = ("seq", "hid")
VMEM_BYTES = 56 << 20
SMALL_VMEM_BYTES = 24 << 20
LIGHT = pl.CostEstimate(flops=1, bytes_accessed=1, transcendentals=0)


def place(device):
    hid = device % 2
    seq = device // 2
    return seq // 32, seq // 8 % 4, seq // 2 % 4, seq % 2, hid


def device_at(x_lo, z, y, core, hid):
    return (((x_lo * 4 + z % 4) * 4 + y % 4) * 2 + core) * 2 + hid


def moved(value, target):
    pairs = []
    for device in range(128):
        there = target(*place(device))
        if there is not None:
            pairs.append((device, there))
    return lax.ppermute(value, AXES, pairs)


def after(value, *others):
    return lax.optimization_barrier((value, *others))[0]


def to_partner_core(x_lo, z, y, core, hid):
    return device_at(x_lo, z, y, 1 - core, hid)


def to_next_frame(x_lo, z, y, core, hid):
    chip = (x_lo * 4 + z) * 4 + y + (1 if core == 0 else -1)
    if not 0 <= chip < 32:
        return None
    return (chip * 2 + core) * 2 + hid


def along_y(x_lo, z, y, core, hid):
    return device_at(x_lo, z, y + (1 if core == 0 else -1), core, hid)


def along_z(x_lo, z, y, core, hid):
    return device_at(x_lo, z + (1 if core == 0 else -1), y, core, hid)


def along_x(x_lo, z, y, core, hid):
    return device_at(1 - x_lo, z, y, core, hid)


def to_other_hid(x_lo, z, y, core, hid):
    return device_at(x_lo, z, y, core, 1 - hid)


def to_other_hid_crossed(x_lo, z, y, core, hid):
    return device_at(x_lo, z, y, 1 - core, 1 - hid)


def attend_kernel(bias_ref, q_ref, res_ref, *refs):
    pairs, out_ref = refs[:3], refs[3]
    tiles = [(ref, row) for ref in pairs for row in (0, TILE)]
    for head in range(q_ref.shape[1] // HEAD_DIM):
        cols = slice(head * HEAD_DIM, (head + 1) * HEAD_DIM)
        query = q_ref[:, cols]
        scores = []
        tops = []
        for t, (ref, row) in enumerate(tiles):
            s = lax.dot_general(
                query, ref[row : row + TILE, cols], (((1,), (1,)), ((), ())), preferred_element_type=jnp.float32
            )
            scores.append(s)
            tops.append(jnp.max(s, axis=-1, keepdims=True) + bias_ref[t])
        top = functools.reduce(jnp.maximum, tops) * LOG2_SCALE
        total = None
        blended = None
        for t, (ref, row) in enumerate(tiles):
            probs = jnp.exp2(scores[t] * LOG2_SCALE + (bias_ref[t] - top))
            row_sum = jnp.sum(probs, axis=-1, keepdims=True)
            part = jnp.dot(
                probs.astype(jnp.bfloat16),
                ref[2 * TILE + row : 3 * TILE + row, cols],
                preferred_element_type=jnp.float32,
            )
            total = row_sum if total is None else total + row_sum
            blended = part if blended is None else blended + part
        attn = (blended / total).astype(jnp.bfloat16)
        out_ref[:, cols] = (res_ref[:, cols].astype(jnp.float32) + attn.astype(jnp.float32)).astype(
            jnp.bfloat16
        )


def attend(bias, queries, residual, both, mine, theirs, first, near, heads):
    wide = 2 * HEAD_DIM
    tall = lambda rows, at: pl.BlockSpec((rows, wide), lambda i: (0, at // 2 + i))
    return pl.pallas_call(
        attend_kernel,
        out_shape=jax.ShapeDtypeStruct((TILE, heads * HEAD_DIM), jnp.bfloat16),
        grid=(heads // 2,),
        in_specs=[pl.BlockSpec(memory_space=pltpu.SMEM)] + [tall(TILE, first)] * 2 + [tall(4 * TILE, near)] * 3,
        out_specs=tall(TILE, 0),
        compiler_params=pltpu.CompilerParams(vmem_limit_bytes=SMALL_VMEM_BYTES),
        cost_estimate=LIGHT,
        name="attend",
    )(bias, queries, residual, both, mine, theirs)


def gelu(x):
    return 0.5 * x * (1.0 + jnp.tanh(math.sqrt(2.0 / math.pi) * (x + 0.044715 * (x * x * x))))


def scaled_features(hid, groups, first, scale_ref, held_ref):
    square = None
    at = 0
    for half, group in zip((hid, 1 - hid), groups):
        feature = first
        for ref in group:
            width = ref.shape[1]
            gain = 1.0 + scale_ref[:, pl.ds(pl.multiple_of(half * HALF + feature, 128), width)]
            wide = ref[...].astype(jnp.float32)
            held_ref[:, at : at + width] = (wide * gain).astype(jnp.bfloat16)
            part = jnp.sum(wide * wide, axis=-1, keepdims=True)
            square = part if square is None else square + part
            feature += width
            at += width
    return square


def project_in_kernel(counts, blocks, first, has_earlier, is_last, hid_ref, *refs):
    own, other = refs[: counts[0]], refs[counts[0] : sum(counts)]
    scale_ref, *refs = refs[sum(counts) :]
    weights, refs = refs[:blocks], list(refs[blocks:])
    acc_ref, earlier_square_ref = (refs.pop(0), refs.pop(0)) if has_earlier else (None, None)
    out_ref = refs.pop(0)
    square_ref, held_ref = refs

    @pl.when(pl.program_id(0) == 0)
    def _():
        square = scaled_features(hid_ref[0], (own, other), first, scale_ref, held_ref)
        square_ref[...] = square + earlier_square_ref[...] if has_earlier else square

    rows = weights[0].shape[0]
    inner = acc_ref[...] if has_earlier else None
    for i, w_ref in enumerate(weights):
        part = jnp.dot(held_ref[:, i * rows : (i + 1) * rows], w_ref[...], preferred_element_type=jnp.float32)
        inner = part if inner is None else inner + part
    if is_last:
        factor = lax.rsqrt(square_ref[...] * (1.0 / FEAT) + 1e-6)
        out_ref[...] = gelu(inner * factor).astype(jnp.bfloat16)
    else:
        out_ref[...] = inner


def project_in(hid, own, other, first, rows, mod_scale, w_in, earlier=None, is_last=False):
    cols = 512
    depths = [sum(v.shape[1] for v in group) for group in (own, other)]
    blocks = [(half, i) for half, depth in enumerate(depths) for i in range(depth // rows)]
    assert first % rows == 0 and HALF % rows == 0 and all(depth % rows == 0 for depth in depths)
    whole = lambda v: pl.BlockSpec(v.shape, lambda i, h: (0, 0))
    column = pl.BlockSpec((TILE, cols), lambda i, h: (0, i))
    one = jax.ShapeDtypeStruct((TILE, 1), jnp.float32)
    scale = mod_scale.reshape(1, FEAT)

    def block(half, i):
        at = first // rows + i
        return pl.BlockSpec((rows, cols), lambda j, h: ((h[0] if half == 0 else 1 - h[0]) * (HALF // rows) + at, j))

    in_specs = [whole(v) for v in own + other] + [whole(scale)]
    in_specs += [block(half, i) for half, i in blocks]
    operands = [*own, *other, scale] + [w_in] * len(blocks)
    scratch = [pltpu.VMEM((TILE, sum(depths)), jnp.bfloat16)]
    if earlier is not None:
        in_specs += [column, whole(one)]
        operands += earlier
    if is_last:
        out_shape, out_specs = jax.ShapeDtypeStruct((TILE, UNITS), jnp.bfloat16), column
        scratch.insert(0, pltpu.VMEM((TILE, 1), jnp.float32))
    else:
        out_shape = (jax.ShapeDtypeStruct((TILE, UNITS), jnp.float32), one)
        out_specs = (column, whole(one))
    return pl.pallas_call(
        functools.partial(project_in_kernel, (len(own), len(other)), len(blocks), first, earlier is not None, is_last),
        out_shape=out_shape,
        grid_spec=pltpu.PrefetchScalarGridSpec(
            num_scalar_prefetch=1,
            grid=(UNITS // cols,),
            in_specs=in_specs,
            out_specs=out_specs,
            scratch_shapes=scratch,
        ),
        compiler_params=pltpu.CompilerParams(vmem_limit_bytes=VMEM_BYTES),
        cost_estimate=LIGHT,
        name="project_in",
    )(hid, *operands)


def project_out_kernel(part_ref, hidden_ref, w_ref, out_ref):
    out_ref[...] = lax.dot_general(
        hidden_ref[...], w_ref[...], (((1,), (1,)), ((), ())), preferred_element_type=jnp.float32
    ).astype(out_ref.dtype)


def project_out(part, hidden, w_rows, dtype):
    cols = 256
    return pl.pallas_call(
        project_out_kernel,
        out_shape=jax.ShapeDtypeStruct((TILE, QUARTER), dtype),
        grid_spec=pltpu.PrefetchScalarGridSpec(
            num_scalar_prefetch=1,
            grid=(QUARTER // cols,),
            in_specs=[
                pl.BlockSpec((TILE, UNITS), lambda i, p: (0, 0)),
                pl.BlockSpec((cols, UNITS), lambda i, p: (p[0] * (QUARTER // cols) + i, 0)),
            ],
            out_specs=pl.BlockSpec((TILE, cols), lambda i, p: (0, i)),
        ),
        compiler_params=pltpu.CompilerParams(vmem_limit_bytes=VMEM_BYTES),
        cost_estimate=LIGHT,
        name="project_out",
    )(part, hidden, w_rows)


def finish_kernel(chunk_count, core_ref, *refs):
    combined = refs[:chunk_count]
    kept_there, kept_here, received_here, received_there, gate_ref, out_ref = refs[chunk_count:]

    def write(core):
        at = 0
        for ref in combined:
            for left in range(0, ref.shape[1], 256):
                cols = slice(at + left, at + left + 256)
                near = slice(cols.start % QUARTER, cols.start % QUARTER + 256)
                if cols.start // QUARTER == core:
                    mlp = kept_there[:, near].astype(jnp.float32) + received_here[:, near].astype(jnp.float32)
                else:
                    mlp = kept_here[:, near] + received_there[:, near].astype(jnp.float32)
                wide = ref[:, left : left + 256].astype(jnp.float32)
                out_ref[:, cols] = (wide + gate_ref[:, cols] * mlp).astype(jnp.bfloat16)
            at += ref.shape[1]

    for core in (0, 1):
        pl.when(core_ref[0] == core)(functools.partial(write, core))


def finish(core, combined, kept_there, kept_here, received_here, received_there, gate):
    vmem = pl.BlockSpec(memory_space=pltpu.VMEM)
    return pl.pallas_call(
        functools.partial(finish_kernel, len(combined)),
        out_shape=jax.ShapeDtypeStruct((TILE, HALF), jnp.bfloat16),
        in_specs=[pl.BlockSpec(memory_space=pltpu.SMEM)] + [vmem] * (len(combined) + 5),
        out_specs=vmem,
        compiler_params=pltpu.CompilerParams(vmem_limit_bytes=SMALL_VMEM_BYTES),
        cost_estimate=LIGHT,
        name="finish",
    )(core, *combined, kept_there, kept_here, received_here, received_there, gate)


def on_device(
    queries, keys, values, residual, w_in, w_out, mod_scale, mod_gate, slot_tiles, key_tiles
):
    seq = lax.axis_index("seq")
    hid = lax.axis_index("hid")
    core = seq % 2
    y = seq // 2 % 4
    z = seq // 8 % 4
    x_lo = seq // 32

    side = 1 - 2 * core
    slots = seq + side * jnp.array([0, 1, -2, -1, 3, 2], jnp.int32)
    inside = (slots >= 0) & (slots < slot_tiles.shape[0])
    tiles = slot_tiles[jnp.clip(slots, 0, slot_tiles.shape[0] - 1)]
    listed = jnp.any(key_tiles[slot_tiles[seq]][:, None] == tiles[None, :], axis=0)
    bias = jnp.where(listed & inside, 0.0, -jnp.inf).astype(jnp.float32)

    counts = FRAME_CHUNKS
    starts = [sum(counts[:i]) for i in range(len(counts))]
    swap = lambda v: moved(v, to_partner_core)
    join = lambda *v: jnp.concatenate(v, axis=0)
    hid_1 = hid.reshape(1)
    mine, own, others, theirs, both = [], [], [], [], []

    def pack(i):
        cols = slice(starts[i] * HEAD_DIM, (starts[i] + counts[i]) * HEAD_DIM)
        return join(keys[:, cols], values[:, cols])

    def send_frame(here, there):
        both.append(join(here[:TILE], there[:TILE], here[TILE:], there[TILE:]))
        mine.append(moved(both[-1], to_next_frame))
        return both[-1]

    def attend_heads(i, near, heads, *earlier):
        part = attend(
            after(bias, *earlier),
            queries,
            residual,
            both[i],
            mine[i],
            theirs[i],
            starts[i] + near,
            near,
            heads,
        )
        own.append(part)
        others.append(moved(part, to_other_hid))
        return part

    own_is_other_half = x_lo == 1 - hid
    gives_other_half = (core == 0) == (z < 2)
    same = [[32 * x + 2 * i + c for i in range(16)] for x in (0, 1) for c in (0, 1)]
    piece = w_out.T
    piece_x = moved(piece, along_x)
    pack_0 = after(pack(0), piece)
    other_0 = swap(pack_0)
    piece_x = after(piece_x, pack_0)
    w_hold = jnp.where(own_is_other_half == gives_other_half, piece, piece_x)
    w_pass = jnp.where(own_is_other_half == gives_other_half, piece_x, piece)
    w_take = swap(w_pass)
    done = send_frame(pack_0, after(other_0, w_pass))
    w_take = after(w_take, done)
    w_chip = join(jnp.where(core == 0, w_hold, w_take), jnp.where(core == 0, w_take, w_hold))
    w_rows = lax.all_gather(w_chip, "seq", axis=0, tiled=True, axis_index_groups=same)
    pack_1 = after(pack(1), w_chip)
    other_1 = swap(pack_1)
    done = send_frame(pack_1, other_1)
    mine[0] = after(mine[0], done)
    theirs.append(swap(mine[0]))
    done = attend_heads(0, 0, 8)
    mine[1] = after(mine[1], done)
    theirs.append(swap(mine[1]))
    done = attend_heads(1, 0, 4)
    earlier = project_in(after(hid_1, done), own, [], 0, HALF, mod_scale, w_in)
    hidden = project_in(hid_1, [], others, 0, HALF, mod_scale, w_in, earlier, is_last=True)
    hidden_there = swap(hidden)
    core_1 = core.reshape(1)
    sent_here = project_out(core_1, hidden, w_rows, jnp.bfloat16)
    received_here = moved(sent_here, to_other_hid)
    hidden_there = after(hidden_there, sent_here)
    sent_there = project_out(core_1, hidden_there, w_rows, jnp.bfloat16)
    received_there = moved(sent_there, to_other_hid_crossed)
    kept_there = project_out(after(1 - core_1, sent_there), hidden_there, w_rows, jnp.bfloat16)
    kept_here = project_out(after(1 - core_1, kept_there), hidden, w_rows, jnp.float32)
    kept_there = jnp.concatenate((swap(kept_there[:, :384]), swap(kept_there[:, 384:])), axis=1)
    gate = lax.dynamic_slice_in_dim(mod_gate, hid * HALF, HALF).reshape(1, HALF)
    return finish(core_1, own, kept_there, kept_here, received_here, received_there, gate)


def solution(mesh):
    placed = (
        P("seq", "hid"),
        P("seq", "hid"),
        P("seq", "hid"),
        P("seq", "hid"),
        P(None, "hid"),
        P("hid", "seq"),
        P(),
        P(),
        P(),
        P(),
    )
    return jax.shard_map(
        on_device, mesh=mesh, in_specs=placed, out_specs=P("seq", "hid"), check_vma=False
    )
```
